256 devices in a mesh: gz: 4 (over y_hi, core), xy: 64 (over y_lo, z, x).
Axes of the slice: x: 4, y: 4 (y_hi: 2, y_lo: 2; y = y_hi * 2 + y_lo), z: 8, core: 2. Of those that a mesh axis runs over, the one named last changes fastest.
Arguments:
- images: bfloat16 [64, 8192, 256], P('gz', 'xy')
- offsets: int32 [128, 4, 2], P('xy'), may hold values from 0 to 63, as said below
- gaps: int32 [64], P('gz'), may hold values from 1 to 2
Outputs:
- smoothed_field: float32 [2, 64, 128, 4], P(None, 'gz', 'xy')
- composed_field: float32 [2, 64, 128, 4], P(None, 'gz', 'xy')
The draws below stay inside these ranges and needn't reach their ends.
Inputs may be any that keep to these rules, and one draw needn't show every extreme that they name: `offsets`: for patch rows r with r mod 2 == 0 the row offset is below 16; for r mod 2 == 1 it is 48 or more.
All inputs are finite; a program needn't handle non-finite values.
Results may differ from the reference program's by a relative error of at most 0.0043.
Values may be sent and summed in bfloat16 or wider, within the bound.
No kernel may reach another device: no remote copies, remote signals or barrier semaphores. Data moves between devices by JAX's collectives and lax.ppermute only.
A program may use at most 64 MiB of HBM per device.

```python
import math
import jax
import jax.numpy as jnp
from jax import lax

P_SIZE = 64
HALF = 32
W = 256
GR = 2
GC = 4
SECTIONS = 64
NROWS = 8192
GROWS = 128


def draw_images(key, part):
    key = jax.random.fold_in(key, 7)
    base_key, shift_key, noise_key = jax.random.split(key, 3)
    base = jax.random.normal(base_key, (NROWS + 32, W + 32), jnp.float32)
    shifts = jax.random.randint(shift_key, (SECTIONS, 2, NROWS // P_SIZE, W // P_SIZE), 0, 33)
    amplitude = jnp.ones((NROWS // P_SIZE, W // P_SIZE), jnp.float32)
    limit = 6.0
    amp_pixels = jnp.repeat(jnp.repeat(amplitude, P_SIZE, 0), P_SIZE, 1)
    row_index = jnp.arange(NROWS, dtype=jnp.int32)
    col_index = jnp.arange(W, dtype=jnp.int32)

    def draw_section(index):
        shift_rows = jnp.repeat(jnp.repeat(shifts[index, 0], P_SIZE, 0), P_SIZE, 1)
        shift_cols = jnp.repeat(jnp.repeat(shifts[index, 1], P_SIZE, 0), P_SIZE, 1)
        common = base[row_index[:, None] + shift_rows, col_index[None, :] + shift_cols]
        noise_part = jax.random.normal(jax.random.fold_in(noise_key, index), (NROWS, W), jnp.float32)
        return jnp.clip((0.8 * common + 0.6 * noise_part) * amp_pixels, -limit, limit)
    return lax.map(draw_section, jnp.arange(SECTIONS, dtype=jnp.int32)).astype(jnp.bfloat16)


def draw_offsets(key, part):
    key = jax.random.fold_in(key, 11)
    any_key, low_key, high_key, col_key = jax.random.split(key, 4)
    row_any = jax.random.randint(any_key, (GROWS, GC), 0, P_SIZE)
    row_low = jax.random.randint(low_key, (GROWS, GC), 0, HALF // 2)
    row_high = jax.random.randint(high_key, (GROWS, GC), HALF + HALF // 2, P_SIZE)
    local_row = (jnp.arange(GROWS, dtype=jnp.int32) % GR)[:, None]
    row_part = jnp.where(local_row == 0, row_low, jnp.where(local_row == GR - 1, row_high, row_any))
    col_part = jax.random.randint(col_key, (GROWS, GC), 0, P_SIZE)
    return jnp.stack([row_part, col_part], -1).astype(jnp.int32)


def plant(array, key, smallest, largest):
    place = [jax.random.randint(jax.random.fold_in(key, axis), (), 0, length) for axis, length in enumerate(array.shape)]
    longest = array.shape.index(max(array.shape))
    neighbour = place[:longest] + [(place[longest] + 1) % array.shape[longest]] + place[longest + 1:]
    return array.at[tuple(place)].set(smallest).at[tuple(neighbour)].set(largest)


def setup_inputs(seed: int = 0) -> dict:
    keys = jax.random.split(jax.random.key(seed), 4)
    images = draw_images(jax.random.fold_in(keys[3], 71), 0)
    offsets = draw_offsets(jax.random.fold_in(keys[3], 71), 0)
    gaps = plant(jax.random.randint(keys[2], (SECTIONS,), 1, 3), jax.random.fold_in(keys[2], 1), 1, 2).astype(jnp.int32)
    return dict(images=images, offsets=offsets, gaps=gaps)


SHARPNESS = 16.0


def tables():
    indices = jnp.arange(P_SIZE, dtype=jnp.int32)
    product = (indices[:, None] * indices[None, :]) % P_SIZE
    angles = product.astype(jnp.float32) * (2.0 * math.pi / P_SIZE)
    return jnp.cos(angles).astype(jnp.bfloat16), jnp.sin(angles).astype(jnp.bfloat16)


def cut_patches(padded, offsets):
    grid_rows = offsets.shape[0]
    grid_cols = offsets.shape[1]
    row_start = jnp.arange(grid_rows, dtype=jnp.int32)[:, None] * P_SIZE + offsets[:, :, 0]
    col_start = jnp.arange(grid_cols, dtype=jnp.int32)[None, :] * P_SIZE + offsets[:, :, 1]

    def take_patch(row_at, col_at):
        return lax.dynamic_slice(padded, (row_at.astype(jnp.int32), col_at.astype(jnp.int32)), (P_SIZE, P_SIZE))

    return jax.vmap(take_patch)(row_start.reshape(-1), col_start.reshape(-1))


def forward(patches, cos_t, sin_t):
    total = patches.shape[0]
    row_pair = jnp.concatenate([cos_t, sin_t], 1)
    segment_one = jnp.dot(patches.reshape(total * P_SIZE, P_SIZE), row_pair, preferred_element_type=jnp.float32)
    segment_one = segment_one.astype(jnp.bfloat16).reshape(total, P_SIZE, 2 * P_SIZE)
    col_pair = jnp.concatenate([cos_t, sin_t], 0)
    blocks = jnp.einsum('kp,npq->nkq', col_pair.astype(jnp.float32), segment_one.astype(jnp.float32))
    real_part = blocks[:, :P_SIZE, :P_SIZE] - blocks[:, P_SIZE:, P_SIZE:]
    imag_part = -(blocks[:, :P_SIZE, P_SIZE:] + blocks[:, P_SIZE:, :P_SIZE])
    return jnp.concatenate([real_part, imag_part], -1).astype(jnp.bfloat16)


def correlate(partner, current, cos_t, sin_t):
    total = partner.shape[0]
    part_re = partner[:, :, :P_SIZE].astype(jnp.float32)
    part_im = partner[:, :, P_SIZE:].astype(jnp.float32)
    own_re = current[:, :, :P_SIZE].astype(jnp.float32)
    own_im = current[:, :, P_SIZE:].astype(jnp.float32)
    cross_re = part_re * own_re + part_im * own_im
    cross_im = part_re * own_im - part_im * own_re
    cross = jnp.concatenate([cross_re, cross_im], -1).astype(jnp.bfloat16)
    col_pair = jnp.concatenate([cos_t, sin_t], 0)
    blocks = jnp.einsum('kp,npq->nkq', col_pair.astype(jnp.float32), cross.astype(jnp.float32))
    mixed_re = blocks[:, :P_SIZE, :P_SIZE] - blocks[:, P_SIZE:, P_SIZE:]
    mixed_im = blocks[:, :P_SIZE, P_SIZE:] + blocks[:, P_SIZE:, :P_SIZE]
    segment_two = jnp.concatenate([mixed_re, mixed_im], -1).astype(jnp.bfloat16)
    back_table = jnp.concatenate([cos_t, -sin_t], 0)
    correlation = jnp.dot(segment_two.reshape(total * P_SIZE, 2 * P_SIZE), back_table, preferred_element_type=jnp.float32)
    scores = correlation.reshape(total, P_SIZE * P_SIZE) * (SHARPNESS / (P_SIZE * P_SIZE * P_SIZE * P_SIZE))
    weights = jax.nn.softmax(scores, axis=-1).reshape(total, P_SIZE, P_SIZE)
    indices = jnp.arange(P_SIZE, dtype=jnp.int32)
    signed = jnp.where(indices < HALF, indices, indices - P_SIZE).astype(jnp.float32)
    shift_rows = jnp.sum(jnp.sum(weights, axis=2) * signed[None, :], axis=1) / 8.0
    shift_cols = jnp.sum(jnp.sum(weights, axis=1) * signed[None, :], axis=1) / 8.0
    return shift_rows, shift_cols


def relaxed_step(values):
    padded = jnp.pad(values, ((0, 0), (0, 0), (1, 1), (1, 1)))
    middle = padded[:, :, 1:-1, 1:-1]
    beside_all = padded[:, :, :-2, 1:-1] + padded[:, :, 2:, 1:-1] + padded[:, :, 1:-1, :-2] + padded[:, :, 1:-1, 2:]
    return 0.5 * middle + 0.125 * beside_all


def reference(images, offsets, gaps):
    cos_t, sin_t = tables()
    patch_count = offsets.shape[0] * offsets.shape[1]

    def advance(carried, inputs):
        older_spec, newer_spec = carried
        section_image, gap_now = inputs
        padded = jnp.pad(section_image, ((HALF, HALF), (HALF, HALF)))
        current = forward(cut_patches(padded, offsets), cos_t, sin_t)
        partner = jnp.where(gap_now == 1, newer_spec, older_spec)
        shift_rows, shift_cols = correlate(partner, current, cos_t, sin_t)
        return (newer_spec, current), jnp.stack([shift_rows, shift_cols])

    empty = jnp.zeros((patch_count, P_SIZE, 2 * P_SIZE), jnp.bfloat16)
    carried, measured = lax.scan(advance, (empty, empty), (images, gaps))
    measured = jnp.transpose(measured, (1, 0, 2)).reshape(2, SECTIONS, GROWS, GC)
    smoothed_field = relaxed_step(relaxed_step(measured))
    composed_field = jnp.cumsum(smoothed_field, axis=1)
    return smoothed_field, composed_field
```

```python
import math

import jax
import jax.numpy as jnp
import ml_dtypes
import numpy as np
from jax import lax
from jax.experimental import pallas as pl
from jax.experimental.pallas import tpu as pltpu
from jax.sharding import PartitionSpec as P

P_SIZE = 64
HALF = 32
SHARPNESS = 16.0
WIN = 128
GR = 2
GC = 4
PATCHES = GR * GC


def shifted(value, axis, steps):
    count = lax.axis_size(axis)
    initial, last = (max(0, -steps), min(count, count - steps))
    return lax.ppermute(value, axis, [(source, source + steps) for source in range(initial, last)])


def tables():
    indices = np.arange(P_SIZE)
    angles = (indices[:, None] * indices[None, :] % P_SIZE) * (2.0 * math.pi / P_SIZE)
    cos_t = np.cos(angles).astype(np.float32).astype(ml_dtypes.bfloat16).astype(np.float32)
    sin_t = np.sin(angles).astype(np.float32).astype(ml_dtypes.bfloat16).astype(np.float32)
    sin_t = np.where(np.abs(sin_t) < 1e-6, np.float32(0), sin_t)
    return cos_t, sin_t


def make_constants():
    cos_t, sin_t = tables()
    zero = np.zeros((P_SIZE, P_SIZE), np.float32)
    cols = np.zeros((2 * P_SIZE, 256), np.float32)
    cols[:P_SIZE, :P_SIZE] = cos_t
    cols[P_SIZE:, :P_SIZE] = sin_t
    from_u = np.concatenate([cos_t, -sin_t, -sin_t, cos_t], 1)
    from_v = np.concatenate([-sin_t, -cos_t, -cos_t, -sin_t], 1)
    edge = np.zeros((P_SIZE, 256), np.float32)
    rows = np.stack([np.concatenate([t, edge], 0) for t in (from_u, from_v)])
    to_re = np.concatenate([cos_t, cos_t, -sin_t, sin_t], 0)
    to_im = np.concatenate([sin_t, sin_t, cos_t, -cos_t], 0)
    blank = np.zeros_like(to_re)
    back_k = np.concatenate(
        [
            np.concatenate([to_re, blank, to_im, blank], 1),
            np.concatenate([blank, to_re, blank, to_im], 1),
        ],
        0,
    )
    scale = SHARPNESS / P_SIZE**4
    back_l = np.concatenate([cos_t, -sin_t], 1) * np.float32(scale)
    bf = ml_dtypes.bfloat16
    return cols, rows, back_k.astype(bf), back_l.astype(bf)


def patch_kernel(
    off_ref, gap_ref, own_ref, prior_ref, low_ref, high_ref, cols_ref, rows_ref, back_k_ref, back_l_ref,
    out_ref, m_ref, x_ref, w_ref, z_ref, ab_ref, g_ref, max_ref, sum_ref, mom_ref,
):
    sections = own_ref.shape[0]
    stacked = sections + 2
    f32 = jnp.float32
    bf16 = jnp.bfloat16
    lane = lax.broadcasted_iota(jnp.int32, (2 * P_SIZE, 256), 1)
    for r in range(GR):
        for c in range(GC):
            i = r * GC + c
            row_at = off_ref[r, c, 0]
            start = c * P_SIZE - HALF + off_ref[r, c, 1]
            turn = jnp.where(start < 0, start + 256, start)
            turned = pltpu.roll(cols_ref[...], turn, 1)
            inside = (lane >= start) & (lane < start + P_SIZE)
            m_ref[r, c * 128 : (c + 1) * 128, :] = jnp.where(inside, turned, 0.0).astype(bf16)
            for half in range(2):
                w_ref[i, half * WIN : (half + 1) * WIN, :] = pltpu.roll(rows_ref[half], row_at, 0).astype(bf16)

    def window(r, t):
        image = prior_ref.at[t] if t < 2 else own_ref.at[t - 2]
        if r == 0:
            return [low_ref[t], image[: WIN - HALF]]
        return [image[HALF:], high_ref[t]]

    for r in range(GR):
        for pair in range(stacked // 2):
            both = jnp.concatenate(window(r, 2 * pair) + window(r, 2 * pair + 1), 0)
            first = lax.dot_general(m_ref[r], both, (((1,), (1,)), ((), ())), preferred_element_type=f32)
            first = first.astype(bf16)
            for c in range(GC):
                for half in range(2):
                    for k in range(2):
                        t = 2 * pair + k
                        x_ref[r * GC + c, t * 64 : (t + 1) * 64, half * WIN : (half + 1) * WIN] = first[
                            c * 128 + half * 64 : c * 128 + (half + 1) * 64, k * WIN : (k + 1) * WIN
                        ]

    signed = lax.broadcasted_iota(jnp.int32, (P_SIZE, sections * P_SIZE), 0)
    signed = jnp.where(signed < HALF, signed, signed - P_SIZE).astype(f32)

    def one_patch(i, carry):
        z_ref[...] = jnp.dot(x_ref[i], w_ref[i], preferred_element_type=f32).astype(bf16)
        for s in range(sections):
            at = pl.multiple_of((s + 2 - gap_ref[s]) * 64, 64)
            partner = z_ref[pl.ds(at, 64), 0:128]
            row, col = (s // 2) * 64, (s % 2) * 256
            ab_ref[row : row + 64, col : col + 128] = partner * z_ref[(s + 2) * 64 : (s + 3) * 64, 0:128]
            ab_ref[row : row + 64, col + 128 : col + 256] = partner * z_ref[(s + 2) * 64 : (s + 3) * 64, 128:256]
        mixed = jnp.dot(ab_ref[...], back_k_ref[...], preferred_element_type=f32).astype(bf16)
        for pair in range(sections // 2):
            g_ref[0:64, pair * 128 : (pair + 1) * 128] = mixed[pair * 64 : (pair + 1) * 64, 0:128]
            g_ref[64:128, pair * 128 : (pair + 1) * 128] = mixed[pair * 64 : (pair + 1) * 64, 128:256]
        scores = jnp.dot(back_l_ref[...], g_ref[...], preferred_element_type=f32)
        top = jnp.max(scores, axis=0, keepdims=True)
        weights = jnp.exp(scores - top)
        max_ref[pl.ds(i, 1), :] = top
        sum_ref[pl.ds(i, 1), :] = jnp.sum(weights, axis=0, keepdims=True)
        mom_ref[pl.ds(i, 1), :] = jnp.sum(weights * signed, axis=0, keepdims=True)
        return carry

    lax.fori_loop(0, PATCHES, one_patch, 0)

    lane = lax.broadcasted_iota(jnp.int32, (PATCHES, 128), 1)
    left = lane < 64
    shift = lane % 64
    shift = jnp.where(shift < HALF, shift, shift - P_SIZE).astype(f32)
    place = lax.broadcasted_iota(jnp.int32, (PATCHES, sections), 1)
    rows_out = jnp.zeros((PATCHES, sections), f32)
    cols_out = jnp.zeros((PATCHES, sections), f32)
    for pair in range(sections // 2):
        part = slice(pair * 128, (pair + 1) * 128)
        top = max_ref[:, part]
        top_a = jnp.max(jnp.where(left, top, -jnp.inf), axis=1, keepdims=True)
        top_b = jnp.max(jnp.where(left, -jnp.inf, top), axis=1, keepdims=True)
        factor = jnp.exp(top - jnp.where(left, top_a, top_b))
        total = factor * sum_ref[:, part]
        moment = factor * mom_ref[:, part]
        for k in range(2):
            mine = left if k == 0 else jnp.logical_not(left)
            den = jnp.sum(jnp.where(mine, total, 0.0), axis=1, keepdims=True)
            along_u = jnp.sum(jnp.where(mine, total * shift, 0.0), axis=1, keepdims=True)
            along_v = jnp.sum(jnp.where(mine, moment, 0.0), axis=1, keepdims=True)
            here = place == 2 * pair + k
            rows_out = jnp.where(here, along_u / den / 8.0, rows_out)
            cols_out = jnp.where(here, along_v / den / 8.0, cols_out)
    out_ref[0:PATCHES, :] = rows_out
    out_ref[PATCHES:, :] = cols_out


def measure(offsets, gaps, images, prior, low, high):
    sections = images.shape[0]
    stacked = sections + 2
    cols, rows, back_k, back_l = make_constants()
    smem = pl.BlockSpec(memory_space=pltpu.SMEM)
    vmem = pl.BlockSpec(memory_space=pltpu.VMEM)
    bf16 = jnp.bfloat16
    return pl.pallas_call(
        patch_kernel,
        out_shape=jax.ShapeDtypeStruct((2 * PATCHES, sections), jnp.float32),
        in_specs=[smem, smem] + [vmem] * 8,
        out_specs=vmem,
        scratch_shapes=[
            pltpu.VMEM((GR, GC * 128, 256), bf16),
            pltpu.VMEM((PATCHES, stacked * 64, 2 * WIN), bf16),
            pltpu.VMEM((PATCHES, 2 * WIN, 256), bf16),
            pltpu.VMEM((stacked * 64, 256), bf16),
            pltpu.VMEM((sections * 32, 512), bf16),
            pltpu.VMEM((128, sections * 64), bf16),
            pltpu.VMEM((PATCHES, sections * 64), jnp.float32),
            pltpu.VMEM((PATCHES, sections * 64), jnp.float32),
            pltpu.VMEM((PATCHES, sections * 64), jnp.float32),
        ],
        compiler_params=pltpu.CompilerParams(vmem_limit_bytes=48 * 1024 * 1024),
    )(offsets, gaps, images, prior, low, high, cols, rows, back_k, back_l)


def relaxed_step(extended):
    middle = extended[:, 1:-1]
    widened = jnp.pad(middle, ((0, 0), (0, 0), (1, 1), (0, 0)))
    beside = extended[:, :-2] + extended[:, 2:] + widened[:, :, :-2] + widened[:, :, 2:]
    return 0.5 * middle + 0.125 * beside


def local(images, offsets, gaps):
    sections = images.shape[0]
    rows_here = images.shape[1]
    prior = shifted(images[sections - 2 :], "gz", 1)
    top = jnp.concatenate([prior[:, :HALF], images[:, :HALF]], 0)
    bottom = jnp.concatenate([prior[:, rows_here - HALF :], images[:, rows_here - HALF :]], 0)
    low = shifted(bottom, "xy", 1)
    high = shifted(top, "xy", -1)
    measured = measure(offsets, gaps, images, prior, low, high)
    above = shifted(measured, "xy", 1).reshape(2, GR, GC, sections)
    below = shifted(measured, "xy", -1).reshape(2, GR, GC, sections)
    measured = measured.reshape(2, GR, GC, sections)
    wide = relaxed_step(jnp.concatenate([above, measured, below], 1))
    place = lax.axis_index("xy")
    row = place * GR + jnp.arange(-1, GR + 1)
    inside = (row >= 0) & (row < GR * lax.axis_size("xy"))
    wide = jnp.where(inside[None, :, None, None], wide, 0.0)
    smoothed = relaxed_step(wide).transpose(0, 3, 1, 2)
    running = jnp.cumsum(smoothed, axis=1)
    gathered = lax.all_gather(running[:, sections - 1], "gz")
    earlier = jnp.arange(gathered.shape[0]) < lax.axis_index("gz")
    earlier_sum = jnp.sum(jnp.where(earlier[:, None, None, None], gathered, 0.0), axis=0)
    return smoothed, running + earlier_sum[:, None]


def solution(mesh):
    in_specs = (P("gz", "xy", None), P("xy", None, None), P("gz"))
    out_specs = (P(None, "gz", "xy", None), P(None, "gz", "xy", None))
    return jax.shard_map(local, mesh=mesh, in_specs=in_specs, out_specs=out_specs, check_vma=False)
```

```python
import math

import jax
import jax.numpy as jnp
import ml_dtypes
import numpy as np
from jax import lax
from jax.experimental import pallas as pl
from jax.experimental.pallas import tpu as pltpu
from jax.sharding import PartitionSpec as P

P_SIZE = 64
HALF = 32
SHARPNESS = 16.0
WIN = 128
GR = 2
GC = 4
PATCHES = GR * GC


def shifted(value, axis, steps):
    count = lax.axis_size(axis)
    initial, last = (max(0, -steps), min(count, count - steps))
    return lax.ppermute(value, axis, [(source, source + steps) for source in range(initial, last)])


def tables():
    indices = np.arange(P_SIZE)
    angles = (indices[:, None] * indices[None, :] % P_SIZE) * (2.0 * math.pi / P_SIZE)
    cos_t = np.cos(angles).astype(np.float32).astype(ml_dtypes.bfloat16).astype(np.float32)
    sin_t = np.sin(angles).astype(np.float32).astype(ml_dtypes.bfloat16).astype(np.float32)
    sin_t = np.where(np.abs(sin_t) < 1e-6, np.float32(0), sin_t)
    return cos_t, sin_t


def make_constants():
    cos_t, sin_t = tables()
    half = P_SIZE // 2
    cols = np.zeros((P_SIZE + 8, 256), np.float32)
    cols[:half, :P_SIZE] = cos_t[:half]
    cols[half:P_SIZE, :P_SIZE] = sin_t[:half]
    cols[P_SIZE:, :P_SIZE] = cos_t[half]
    from_u = np.concatenate([cos_t, -sin_t, -sin_t, cos_t], 1)
    from_v = np.concatenate([-sin_t, -cos_t, -cos_t, -sin_t], 1)
    edge = np.zeros((P_SIZE, 256), np.float32)
    rows = np.stack([np.concatenate([t, edge], 0) for t in (from_u, from_v)])
    to_re = np.concatenate([cos_t, -sin_t], 0)
    to_im = np.concatenate([sin_t, cos_t], 0)
    blank = np.zeros_like(to_re)
    back_k = np.concatenate(
        [
            np.concatenate([to_re, blank, to_im, blank], 1),
            np.concatenate([blank, to_re, blank, to_im], 1),
        ],
        0,
    )
    weight = np.where(np.arange(half) == 0, 1.0, 2.0).astype(np.float32)
    one = np.concatenate([cos_t[:, :half] * weight, -sin_t[:, :half] * weight], 1)
    one[:, half] = cos_t[:, half]
    scale = SHARPNESS / P_SIZE**4
    back_l = np.kron(np.eye(GC, dtype=np.float32), one * np.float32(scale))
    bf = ml_dtypes.bfloat16
    return cols, rows, back_k.astype(bf), back_l.astype(bf)


def patch_kernel(
    off_ref, gap_ref, own_ref, prior_ref, low_ref, high_ref, cols_ref, rows_ref, back_k_ref, back_l_ref,
    out_ref, m_ref, x_ref, w_ref, z_ref, n_ref, y_ref, g_ref, max_ref, sum_ref, mom_ref,
):
    sections = own_ref.shape[0]
    stacked = sections + 2
    f32 = jnp.float32
    bf16 = jnp.bfloat16
    main = stacked * 32
    lane = lax.broadcasted_iota(jnp.int32, cols_ref.shape, 1)
    for r in range(GR):
        for c in range(GC):
            i = r * GC + c
            row_at = off_ref[r, c, 0]
            start = c * P_SIZE - HALF + off_ref[r, c, 1]
            turn = jnp.where(start < 0, start + 256, start)
            turned = pltpu.roll(cols_ref[...], turn, 1)
            inside = (lane >= start) & (lane < start + P_SIZE)
            turned = jnp.where(inside, turned, 0.0)
            m_ref[r, c * 64 : (c + 1) * 64, :] = turned[:64].astype(bf16)
            m_ref[r, 256 + c * 16 : 256 + (c + 1) * 16, :] = jnp.concatenate([turned[64:]] * 2, 0).astype(bf16)
            for half in range(2):
                w_ref[i, half * WIN : (half + 1) * WIN, :] = pltpu.roll(rows_ref[half], row_at, 0).astype(bf16)

    def window(r, t):
        image = prior_ref.at[t] if t < 2 else own_ref.at[t - 2]
        if r == 0:
            return [low_ref[t], image[: WIN - HALF]]
        return [image[HALF:], high_ref[t]]

    sub = lax.broadcasted_iota(jnp.int32, (8, WIN), 0)
    for r in range(GR):
        nyquist = [[jnp.zeros((8, WIN), f32) for _ in range(3)] for _ in range(GC)]
        for pair in range(stacked // 2):
            both = jnp.concatenate(window(r, 2 * pair) + window(r, 2 * pair + 1), 0)
            first = lax.dot_general(m_ref[r], both, (((1,), (1,)), ((), ())), preferred_element_type=f32)
            for c in range(GC):
                for k in range(2):
                    t = 2 * pair + k
                    for half in range(2):
                        x_ref[r * GC + c, t * 32 : (t + 1) * 32, half * WIN : (half + 1) * WIN] = first[
                            c * 64 + half * 32 : c * 64 + (half + 1) * 32, k * WIN : (k + 1) * WIN
                        ].astype(bf16)
                    block, at = (2, t) if t < 2 else ((t - 2) // 8, (t - 2) % 8)
                    row = first[256 + c * 16 : 264 + c * 16, k * WIN : (k + 1) * WIN]
                    nyquist[c][block] = jnp.where(sub == at, row, nyquist[c][block])
        for c in range(GC):
            i = r * GC + c
            x_ref[i, main : main + 16, :WIN] = jnp.concatenate(nyquist[c][:2], 0).astype(bf16)
            x_ref[i, main + 16 :, :WIN] = jnp.concatenate([nyquist[c][2]] * 2, 0).astype(bf16)
            x_ref[i, main:, WIN:] = jnp.zeros((32, WIN), bf16)

    for i in range(PATCHES):
        z_ref[i] = jnp.dot(x_ref[i], w_ref[i], preferred_element_type=f32).astype(bf16)

    def crossed(partner_p, partner_q, own_p, own_q):
        left = lax.broadcasted_iota(jnp.int32, partner_p.shape, 1) < 64
        twice_re = jnp.where(left, partner_p, partner_q)
        twice_im = jnp.where(left, partner_q, -partner_p)
        return twice_re * own_p + twice_im * own_q

    back = lax.broadcasted_iota(jnp.int32, (16, 128), 0)
    gap_rows = jnp.ones((16, 128), jnp.int32)
    for s in range(sections):
        gap_rows = jnp.where(back == s, gap_ref[s], gap_rows)
    even = back % 2 == 0
    for i in range(PATCHES):
        for s in range(sections):
            at = pl.multiple_of((s + 2 - gap_ref[s]) * 32, 32)
            row = i * 256 + (s // 2) * 32
            y_ref[row : row + 32, (s % 2) * 128 : (s % 2 + 1) * 128] = crossed(
                z_ref[i, pl.ds(at, 32), 0:128],
                z_ref[i, pl.ds(at, 32), 128:256],
                z_ref[i, (s + 2) * 32 : (s + 3) * 32, 0:128],
                z_ref[i, (s + 2) * 32 : (s + 3) * 32, 128:256],
            )
        own = z_ref[i, main : main + 16, :].astype(f32)
        n_ref[i, 8:24, :] = own
        n_ref[i, 0:8, :] = pltpu.roll(z_ref[i, main + 16 : main + 32, :].astype(f32)[0:8], 6, 0)
        one_up = n_ref[i, 7:23, :]
        two_up = n_ref[i, 6:22, :]
        partner_p = jnp.where(gap_rows == 1, one_up[:, :128], two_up[:, :128])
        partner_q = jnp.where(gap_rows == 1, one_up[:, 128:], two_up[:, 128:])
        line = crossed(partner_p, partner_q, own[:, :128], own[:, 128:])
        row = PATCHES * 256 + i * 16
        y_ref[row : row + 16, 0:128] = jnp.where(even, line, 0.0).astype(bf16)
        y_ref[row : row + 16, 128:256] = jnp.where(even, 0.0, line).astype(bf16)

    lines = jnp.dot(y_ref[PATCHES * 256 :, :], back_k_ref[:, :128], preferred_element_type=f32)
    first_row = lax.broadcasted_iota(jnp.int32, (32, 128), 0) == 0
    for i in range(PATCHES):
        mixed = jnp.dot(y_ref[i * 256 : (i + 1) * 256, :], back_k_ref[...], preferred_element_type=f32)
        at = (i % GC) * 64
        for pair in range(sections // 2):
            line = lines[i * 16 + 2 * pair : i * 16 + 2 * pair + 1] + lines[i * 16 + 2 * pair + 1 : i * 16 + 2 * pair + 2]
            part = slice(pair * 128, (pair + 1) * 128)
            g_ref[i // GC, at : at + 32, part] = mixed[pair * 32 : (pair + 1) * 32, 0:128].astype(bf16)
            g_ref[i // GC, at + 32 : at + 64, part] = jnp.where(
                first_row, line, mixed[pair * 32 : (pair + 1) * 32, 128:256]
            ).astype(bf16)

    signed = lax.broadcasted_iota(jnp.int32, (P_SIZE, 256), 0)
    signed = jnp.where(signed < HALF, signed, signed - P_SIZE).astype(f32)
    for r in range(GR):
        for block in range(sections * P_SIZE // 256):
            part = slice(block * 256, (block + 1) * 256)
            all_scores = jnp.dot(back_l_ref[...], g_ref[r, :, part], preferred_element_type=f32)
            for c in range(GC):
                i = r * GC + c
                scores = all_scores[c * 64 : (c + 1) * 64]
                top = jnp.max(scores, axis=0, keepdims=True)
                weights = jnp.exp(scores - top)
                max_ref[i : i + 1, part] = top
                sum_ref[i : i + 1, part] = jnp.sum(weights, axis=0, keepdims=True)
                mom_ref[i : i + 1, part] = jnp.sum(weights * signed, axis=0, keepdims=True)

    lane = lax.broadcasted_iota(jnp.int32, (PATCHES, 128), 1)
    left = lane < 64
    shift = lane % 64
    shift = jnp.where(shift < HALF, shift, shift - P_SIZE).astype(f32)
    place = lax.broadcasted_iota(jnp.int32, (PATCHES, sections), 1)
    rows_out = jnp.zeros((PATCHES, sections), f32)
    cols_out = jnp.zeros((PATCHES, sections), f32)
    for pair in range(sections // 2):
        part = slice(pair * 128, (pair + 1) * 128)
        top = max_ref[:, part]
        top_a = jnp.max(jnp.where(left, top, -jnp.inf), axis=1, keepdims=True)
        top_b = jnp.max(jnp.where(left, -jnp.inf, top), axis=1, keepdims=True)
        factor = jnp.exp(top - jnp.where(left, top_a, top_b))
        total = factor * sum_ref[:, part]
        moment = factor * mom_ref[:, part]
        for k in range(2):
            mine = left if k == 0 else jnp.logical_not(left)
            den = jnp.sum(jnp.where(mine, total, 0.0), axis=1, keepdims=True)
            along_u = jnp.sum(jnp.where(mine, total * shift, 0.0), axis=1, keepdims=True)
            along_v = jnp.sum(jnp.where(mine, moment, 0.0), axis=1, keepdims=True)
            here = place == 2 * pair + k
            rows_out = jnp.where(here, along_u / den / 8.0, rows_out)
            cols_out = jnp.where(here, along_v / den / 8.0, cols_out)
    out_ref[0:PATCHES, :] = rows_out
    out_ref[PATCHES:, :] = cols_out


def measure(offsets, gaps, images, prior, low, high):
    sections = images.shape[0]
    rows_x = (sections + 2) * 32 + 32
    cols, rows, back_k, back_l = make_constants()
    smem = pl.BlockSpec(memory_space=pltpu.SMEM)
    vmem = pl.BlockSpec(memory_space=pltpu.VMEM)
    bf16 = jnp.bfloat16
    f32 = jnp.float32
    return pl.pallas_call(
        patch_kernel,
        out_shape=jax.ShapeDtypeStruct((2 * PATCHES, sections), f32),
        in_specs=[smem, smem] + [vmem] * 8,
        out_specs=vmem,
        scratch_shapes=[
            pltpu.VMEM((GR, 256 + GC * 16, 256), bf16),
            pltpu.VMEM((PATCHES, rows_x, 2 * WIN), bf16),
            pltpu.VMEM((PATCHES, 2 * WIN, 256), bf16),
            pltpu.VMEM((PATCHES, rows_x, 256), bf16),
            pltpu.VMEM((PATCHES, 24, 256), f32),
            pltpu.VMEM((PATCHES * (sections * 16 + 16), 256), bf16),
            pltpu.VMEM((GR, 256, sections * 64), bf16),
            pltpu.VMEM((PATCHES, sections * 64), f32),
            pltpu.VMEM((PATCHES, sections * 64), f32),
            pltpu.VMEM((PATCHES, sections * 64), f32),
        ],
        compiler_params=pltpu.CompilerParams(vmem_limit_bytes=48 * 1024 * 1024),
    )(offsets, gaps, images, prior, low, high, cols, rows, back_k, back_l)


def relaxed_step(extended):
    middle = extended[:, 1:-1]
    widened = jnp.pad(middle, ((0, 0), (0, 0), (1, 1), (0, 0)))
    beside = extended[:, :-2] + extended[:, 2:] + widened[:, :, :-2] + widened[:, :, 2:]
    return 0.5 * middle + 0.125 * beside


def earlier_groups(total):
    place = lax.axis_index("gz")
    count = lax.axis_size("gz")
    other = lax.ppermute(total, "gz", [(i, i ^ 1) for i in range(count)])
    pair = total + other
    before = lax.ppermute(pair, "gz", [(i, i + 2) for i in range(count - 2)])
    return before + jnp.where(place % 2 == 1, other, 0.0)


def local(images, offsets, gaps):
    sections = images.shape[0]
    rows_here = images.shape[1]
    prior = shifted(images[sections - 2 :], "gz", 1)
    top = jnp.concatenate([prior[:, :HALF], images[:, :HALF]], 0)
    bottom = jnp.concatenate([prior[:, rows_here - HALF :], images[:, rows_here - HALF :]], 0)
    low = shifted(bottom, "xy", 1)
    high = shifted(top, "xy", -1)
    measured = measure(offsets, gaps, images, prior, low, high)
    above = shifted(measured, "xy", 1).reshape(2, GR, GC, sections)
    below = shifted(measured, "xy", -1).reshape(2, GR, GC, sections)
    measured = measured.reshape(2, GR, GC, sections)
    wide = relaxed_step(jnp.concatenate([above, measured, below], 1))
    place = lax.axis_index("xy")
    row = place * GR + jnp.arange(-1, GR + 1)
    inside = (row >= 0) & (row < GR * lax.axis_size("xy"))
    wide = jnp.where(inside[None, :, None, None], wide, 0.0)
    smoothed = relaxed_step(wide).transpose(0, 3, 1, 2)
    running = jnp.cumsum(smoothed, axis=1)
    earlier_sum = earlier_groups(running[:, sections - 1])
    return smoothed, running + earlier_sum[:, None]


def solution(mesh):
    in_specs = (P("gz", "xy", None), P("xy", None, None), P("gz"))
    out_specs = (P(None, "gz", "xy", None), P(None, "gz", "xy", None))
    return jax.shard_map(local, mesh=mesh, in_specs=in_specs, out_specs=out_specs, check_vma=False)
```

```python
import math

import jax
import jax.numpy as jnp
import ml_dtypes
import numpy as np
from jax import lax
from jax.experimental import pallas as pl
from jax.experimental.pallas import tpu as pltpu
from jax.sharding import PartitionSpec as P

P_SIZE = 64
HALF = 32
SHARPNESS = 16.0
WIN = 128
GR = 2
GC = 4
PATCHES = GR * GC


def ring(value, axis, steps):
    count = lax.axis_size(axis)
    return lax.ppermute(value, axis, [(source, (source + steps) % count) for source in range(count)])


def tables():
    indices = np.arange(P_SIZE)
    angles = (indices[:, None] * indices[None, :] % P_SIZE) * (2.0 * math.pi / P_SIZE)
    cos_t = np.cos(angles).astype(np.float32).astype(ml_dtypes.bfloat16).astype(np.float32)
    sin_t = np.sin(angles).astype(np.float32).astype(ml_dtypes.bfloat16).astype(np.float32)
    sin_t = np.where(np.abs(sin_t) < 1e-6, np.float32(0), sin_t)
    return cos_t, sin_t


def make_constants():
    cos_t, sin_t = tables()
    half = P_SIZE // 2
    cols = np.zeros((P_SIZE + 8, 256), np.float32)
    cols[:half, :P_SIZE] = cos_t[:half]
    cols[half:P_SIZE, :P_SIZE] = sin_t[:half]
    cols[P_SIZE:, :P_SIZE] = cos_t[half]
    from_u = np.concatenate([cos_t, -sin_t, -sin_t, cos_t], 1)
    from_v = np.concatenate([-sin_t, -cos_t, -cos_t, -sin_t], 1)
    edge = np.zeros((P_SIZE, 256), np.float32)
    rows = np.stack([np.concatenate([t, edge], 0) for t in (from_u, from_v)])
    to_re = np.concatenate([cos_t, -sin_t], 0)
    to_im = np.concatenate([sin_t, cos_t], 0)
    blank = np.zeros_like(to_re)
    back_k = np.concatenate(
        [
            np.concatenate([to_re, blank, to_im, blank], 1),
            np.concatenate([blank, to_re, blank, to_im], 1),
        ],
        0,
    )
    weight = np.where(np.arange(half) == 0, 1.0, 2.0).astype(np.float32)
    one = np.concatenate([cos_t[:, :half] * weight, -sin_t[:, :half] * weight], 1)
    one[:, half] = cos_t[:, half]
    scale = SHARPNESS / P_SIZE**4
    back_l = np.kron(np.eye(GC, dtype=np.float32), one * np.float32(scale))
    bf = ml_dtypes.bfloat16
    return cols, rows, back_k.astype(bf), back_l.astype(bf)


def table_kernel(off_ref, edge_ref, cols_ref, rows_ref, m_ref, w_ref):
    bf16 = jnp.bfloat16
    lane = lax.broadcasted_iota(jnp.int32, cols_ref.shape, 1)
    line = lax.broadcasted_iota(jnp.int32, (WIN, 256), 0)
    for r in range(GR):
        if r == 0:
            inside_image = line >= jnp.where(edge_ref[0] == 1, HALF, 0)
        else:
            inside_image = line < jnp.where(edge_ref[1] == 1, WIN - HALF, WIN)
        for c in range(GC):
            i = r * GC + c
            row_at = off_ref[r, c, 0]
            start = c * P_SIZE - HALF + off_ref[r, c, 1]
            turn = jnp.where(start < 0, start + 256, start)
            turned = pltpu.roll(cols_ref[...], turn, 1)
            inside = (lane >= start) & (lane < start + P_SIZE)
            turned = jnp.where(inside, turned, 0.0)
            m_ref[r, c * 64 : (c + 1) * 64, :] = turned[:64].astype(bf16)
            m_ref[r, 256 + c * 16 : 256 + (c + 1) * 16, :] = jnp.concatenate([turned[64:]] * 2, 0).astype(bf16)
            for half in range(2):
                turned = pltpu.roll(rows_ref[half], row_at, 0)
                w_ref[i, half * WIN : (half + 1) * WIN, :] = jnp.where(inside_image, turned, 0.0).astype(bf16)


def patch_kernel(
    edge_ref, gap_ref, own_ref, prior_ref, low_ref, high_ref, plow_ref, phigh_ref, m_ref, w_ref, back_k_ref, back_l_ref,
    out_ref, x_ref, z_ref, n_ref, y_ref, g_ref, max_ref, sum_ref, mom_ref,
):
    sections = own_ref.shape[0]
    stacked = sections + 2
    f32 = jnp.float32
    bf16 = jnp.bfloat16
    main = stacked * 32
    has_prior = jnp.where(edge_ref[2] == 1, 0.0, 1.0)

    def window(r, t):
        image = prior_ref.at[t] if t < 2 else own_ref.at[t - 2]
        if r == 0:
            return [plow_ref[t] if t < 2 else low_ref[t - 2], image[: WIN - HALF]]
        return [image[HALF:], phigh_ref[t] if t < 2 else high_ref[t - 2]]

    sub = lax.broadcasted_iota(jnp.int32, (8, WIN), 0)
    for r in range(GR):
        nyquist = [[jnp.zeros((8, WIN), f32) for _ in range(3)] for _ in range(GC)]
        for pair in range(stacked // 2):
            both = jnp.concatenate(window(r, 2 * pair) + window(r, 2 * pair + 1), 0)
            first = lax.dot_general(m_ref[r], both, (((1,), (1,)), ((), ())), preferred_element_type=f32)
            if pair == 0:
                first = first * has_prior
            for c in range(GC):
                for k in range(2):
                    t = 2 * pair + k
                    for half in range(2):
                        x_ref[r * GC + c, t * 32 : (t + 1) * 32, half * WIN : (half + 1) * WIN] = first[
                            c * 64 + half * 32 : c * 64 + (half + 1) * 32, k * WIN : (k + 1) * WIN
                        ].astype(bf16)
                    block, at = (2, t) if t < 2 else ((t - 2) // 8, (t - 2) % 8)
                    row = first[256 + c * 16 : 264 + c * 16, k * WIN : (k + 1) * WIN]
                    nyquist[c][block] = jnp.where(sub == at, row, nyquist[c][block])
        for c in range(GC):
            i = r * GC + c
            x_ref[i, main : main + 16, :WIN] = jnp.concatenate(nyquist[c][:2], 0).astype(bf16)
            x_ref[i, main + 16 :, :WIN] = jnp.concatenate([nyquist[c][2]] * 2, 0).astype(bf16)
            x_ref[i, main:, WIN:] = jnp.zeros((32, WIN), bf16)

    for i in range(PATCHES):
        z_ref[i] = jnp.dot(x_ref[i], w_ref[i], preferred_element_type=f32).astype(bf16)

    def crossed(partner_p, partner_q, own_p, own_q):
        left = lax.broadcasted_iota(jnp.int32, partner_p.shape, 1) < 64
        twice_re = jnp.where(left, partner_p, partner_q)
        twice_im = jnp.where(left, partner_q, -partner_p)
        return twice_re * own_p + twice_im * own_q

    back = lax.broadcasted_iota(jnp.int32, (16, 128), 0)
    gap_rows = jnp.ones((16, 128), jnp.int32)
    for s in range(sections):
        gap_rows = jnp.where(back == s, gap_ref[s], gap_rows)
    even = back % 2 == 0
    for i in range(PATCHES):
        for s in range(sections):
            at = pl.multiple_of((s + 2 - gap_ref[s]) * 32, 32)
            row = i * 256 + (s // 2) * 32
            y_ref[row : row + 32, (s % 2) * 128 : (s % 2 + 1) * 128] = crossed(
                z_ref[i, pl.ds(at, 32), 0:128],
                z_ref[i, pl.ds(at, 32), 128:256],
                z_ref[i, (s + 2) * 32 : (s + 3) * 32, 0:128],
                z_ref[i, (s + 2) * 32 : (s + 3) * 32, 128:256],
            )
        own = z_ref[i, main : main + 16, :].astype(f32)
        n_ref[i, 8:24, :] = own
        n_ref[i, 0:8, :] = pltpu.roll(z_ref[i, main + 16 : main + 32, :].astype(f32)[0:8], 6, 0)
        one_up = n_ref[i, 7:23, :]
        two_up = n_ref[i, 6:22, :]
        partner_p = jnp.where(gap_rows == 1, one_up[:, :128], two_up[:, :128])
        partner_q = jnp.where(gap_rows == 1, one_up[:, 128:], two_up[:, 128:])
        line = crossed(partner_p, partner_q, own[:, :128], own[:, 128:])
        row = PATCHES * 256 + i * 16
        y_ref[row : row + 16, 0:128] = jnp.where(even, line, 0.0).astype(bf16)
        y_ref[row : row + 16, 128:256] = jnp.where(even, 0.0, line).astype(bf16)

    lines = jnp.dot(y_ref[PATCHES * 256 :, :], back_k_ref[:, :128], preferred_element_type=f32)
    first_row = lax.broadcasted_iota(jnp.int32, (32, 128), 0) == 0
    for i in range(PATCHES):
        mixed = jnp.dot(y_ref[i * 256 : (i + 1) * 256, :], back_k_ref[...], preferred_element_type=f32)
        at = (i % GC) * 64
        for pair in range(sections // 2):
            line = lines[i * 16 + 2 * pair : i * 16 + 2 * pair + 1] + lines[i * 16 + 2 * pair + 1 : i * 16 + 2 * pair + 2]
            part = slice(pair * 128, (pair + 1) * 128)
            g_ref[i // GC, at : at + 32, part] = mixed[pair * 32 : (pair + 1) * 32, 0:128].astype(bf16)
            g_ref[i // GC, at + 32 : at + 64, part] = jnp.where(
                first_row, line, mixed[pair * 32 : (pair + 1) * 32, 128:256]
            ).astype(bf16)

    signed = lax.broadcasted_iota(jnp.int32, (P_SIZE, 256), 0)
    signed = jnp.where(signed < HALF, signed, signed - P_SIZE).astype(f32)
    for r in range(GR):
        for block in range(sections * P_SIZE // 256):
            part = slice(block * 256, (block + 1) * 256)
            all_scores = jnp.dot(back_l_ref[...], g_ref[r, :, part], preferred_element_type=f32)
            for c in range(GC):
                i = r * GC + c
                scores = all_scores[c * 64 : (c + 1) * 64]
                top = jnp.max(scores, axis=0, keepdims=True)
                weights = jnp.exp(scores - top)
                max_ref[i : i + 1, part] = top
                sum_ref[i : i + 1, part] = jnp.sum(weights, axis=0, keepdims=True)
                mom_ref[i : i + 1, part] = jnp.sum(weights * signed, axis=0, keepdims=True)

    lane = lax.broadcasted_iota(jnp.int32, (PATCHES, 128), 1)
    left = lane < 64
    shift = lane % 64
    shift = jnp.where(shift < HALF, shift, shift - P_SIZE).astype(f32)
    place = lax.broadcasted_iota(jnp.int32, (PATCHES, sections), 1)
    rows_out = jnp.zeros((PATCHES, sections), f32)
    cols_out = jnp.zeros((PATCHES, sections), f32)
    for pair in range(sections // 2):
        part = slice(pair * 128, (pair + 1) * 128)
        top = max_ref[:, part]
        top_a = jnp.max(jnp.where(left, top, -jnp.inf), axis=1, keepdims=True)
        top_b = jnp.max(jnp.where(left, -jnp.inf, top), axis=1, keepdims=True)
        factor = jnp.exp(top - jnp.where(left, top_a, top_b))
        total = factor * sum_ref[:, part]
        moment = factor * mom_ref[:, part]
        for k in range(2):
            mine = left if k == 0 else jnp.logical_not(left)
            den = jnp.sum(jnp.where(mine, total, 0.0), axis=1, keepdims=True)
            along_u = jnp.sum(jnp.where(mine, total * shift, 0.0), axis=1, keepdims=True)
            along_v = jnp.sum(jnp.where(mine, moment, 0.0), axis=1, keepdims=True)
            here = place == 2 * pair + k
            rows_out = jnp.where(here, along_u / den / 8.0, rows_out)
            cols_out = jnp.where(here, along_v / den / 8.0, cols_out)
    out_ref[0:PATCHES, :] = rows_out
    out_ref[PATCHES:, :] = cols_out


def make_tables(offsets, edges):
    cols, rows, _, _ = make_constants()
    smem = pl.BlockSpec(memory_space=pltpu.SMEM)
    vmem = pl.BlockSpec(memory_space=pltpu.VMEM)
    bf16 = jnp.bfloat16
    return pl.pallas_call(
        table_kernel,
        out_shape=(
            jax.ShapeDtypeStruct((GR, 256 + GC * 16, 256), bf16),
            jax.ShapeDtypeStruct((PATCHES, 2 * WIN, 256), bf16),
        ),
        in_specs=[smem, smem, vmem, vmem],
        out_specs=(vmem, vmem),
        compiler_params=pltpu.CompilerParams(vmem_limit_bytes=16 * 1024 * 1024),
        cost_estimate=pl.CostEstimate(flops=4_000_000, bytes_accessed=4_000_000, transcendentals=0),
        name="make_tables",
    )(offsets, edges, cols, rows)


def measure(edges, gaps, images, prior, low, high, plow, phigh, m_table, w_table):
    sections = images.shape[0]
    rows_x = (sections + 2) * 32 + 32
    _, _, back_k, back_l = make_constants()
    smem = pl.BlockSpec(memory_space=pltpu.SMEM)
    vmem = pl.BlockSpec(memory_space=pltpu.VMEM)
    bf16 = jnp.bfloat16
    f32 = jnp.float32
    return pl.pallas_call(
        patch_kernel,
        out_shape=jax.ShapeDtypeStruct((2 * PATCHES, sections), f32),
        in_specs=[smem, smem] + [vmem] * 10,
        out_specs=vmem,
        scratch_shapes=[
            pltpu.VMEM((PATCHES, rows_x, 2 * WIN), bf16),
            pltpu.VMEM((PATCHES, rows_x, 256), bf16),
            pltpu.VMEM((PATCHES, 24, 256), f32),
            pltpu.VMEM((PATCHES * (sections * 16 + 16), 256), bf16),
            pltpu.VMEM((GR, 256, sections * 64), bf16),
            pltpu.VMEM((PATCHES, sections * 64), f32),
            pltpu.VMEM((PATCHES, sections * 64), f32),
            pltpu.VMEM((PATCHES, sections * 64), f32),
        ],
        compiler_params=pltpu.CompilerParams(vmem_limit_bytes=32 * 1024 * 1024),
        cost_estimate=pl.CostEstimate(flops=2_000_000_000, bytes_accessed=6_000_000, transcendentals=600_000),
        name="measure",
    )(edges, gaps, images, prior, low, high, plow, phigh, m_table, w_table, back_k, back_l)


def relaxed_step(extended):
    middle = extended[:, 1:-1]
    widened = jnp.pad(middle, ((0, 0), (0, 0), (1, 1), (0, 0)))
    beside = extended[:, :-2] + extended[:, 2:] + widened[:, :, :-2] + widened[:, :, 2:]
    return 0.5 * middle + 0.125 * beside


def earlier_groups(total):
    place = lax.axis_index("gz")
    count = lax.axis_size("gz")
    other = lax.ppermute(total, "gz", [(i, i ^ 1) for i in range(count)])
    pair = total + other
    across = lax.ppermute(pair, "gz", [(i, (i + 2) % count) for i in range(count)])
    return jnp.where(place >= 2, across, 0.0) + jnp.where(place % 2 == 1, other, 0.0)


def local(images, offsets, gaps):
    sections = images.shape[0]
    rows_here = images.shape[1]
    place = lax.axis_index("xy")
    last = lax.axis_size("xy") - 1
    edges = jnp.stack([place == 0, place == last, lax.axis_index("gz") == 0]).astype(jnp.int32)
    m_table, w_table = make_tables(offsets, edges)
    prior = ring(images[sections - 2 :], "gz", 1)
    low = ring(images[:, rows_here - HALF :], "xy", 1)
    high = ring(images[:, :HALF], "xy", -1)
    plow = ring(prior[:, rows_here - HALF :], "xy", 1)
    phigh = ring(prior[:, :HALF], "xy", -1)
    measured = measure(edges, gaps, images, prior, low, high, plow, phigh, m_table, w_table)
    above = jnp.where(place == 0, 0.0, ring(measured, "xy", 1)).reshape(2, GR, GC, sections)
    below = jnp.where(place == last, 0.0, ring(measured, "xy", -1)).reshape(2, GR, GC, sections)
    measured = measured.reshape(2, GR, GC, sections)
    wide = relaxed_step(jnp.concatenate([above, measured, below], 1))
    row = place * GR + jnp.arange(-1, GR + 1)
    inside = (row >= 0) & (row < GR * (last + 1))
    wide = jnp.where(inside[None, :, None, None], wide, 0.0)
    smoothed = relaxed_step(wide).transpose(0, 3, 1, 2)
    running = jnp.cumsum(smoothed, axis=1)
    earlier_sum = earlier_groups(running[:, sections - 1])
    return smoothed, running + earlier_sum[:, None]


def solution(mesh):
    in_specs = (P("gz", "xy", None), P("xy", None, None), P("gz"))
    out_specs = (P(None, "gz", "xy", None), P(None, "gz", "xy", None))
    return jax.shard_map(local, mesh=mesh, in_specs=in_specs, out_specs=out_specs, check_vma=False)
```

```python
import math

import jax
import jax.numpy as jnp
import ml_dtypes
import numpy as np
from jax import lax
from jax.experimental import pallas as pl
from jax.experimental.pallas import tpu as pltpu
from jax.sharding import PartitionSpec as P

P_SIZE = 64
HALF = 32
SHARPNESS = 16.0
WIN = 128
GR = 2
GC = 4
PATCHES = GR * GC


def ring(value, axis, steps):
    count = lax.axis_size(axis)
    return lax.ppermute(value, axis, [(source, (source + steps) % count) for source in range(count)])


def swap_near(value):
    count = lax.axis_size("xy")
    return lax.ppermute(value, "xy", [(i, i ^ 1) for i in range(count)])


def swap_far(value):
    count = lax.axis_size("xy")
    return lax.ppermute(value, "xy", [(i, (i + 1 if i % 2 else i - 1) % count) for i in range(count)])


def tables():
    indices = np.arange(P_SIZE)
    angles = (indices[:, None] * indices[None, :] % P_SIZE) * (2.0 * math.pi / P_SIZE)
    cos_t = np.cos(angles).astype(np.float32).astype(ml_dtypes.bfloat16).astype(np.float32)
    sin_t = np.sin(angles).astype(np.float32).astype(ml_dtypes.bfloat16).astype(np.float32)
    sin_t = np.where(np.abs(sin_t) < 1e-6, np.float32(0), sin_t)
    return cos_t, sin_t


def make_constants():
    cos_t, sin_t = tables()
    half = P_SIZE // 2
    cols = np.zeros((P_SIZE + 8, 256), np.float32)
    cols[:half, :P_SIZE] = cos_t[:half]
    cols[half:P_SIZE, :P_SIZE] = sin_t[:half]
    cols[P_SIZE:, :P_SIZE] = cos_t[half]
    from_u = np.concatenate([cos_t, -sin_t, -sin_t, cos_t], 1)
    from_v = np.concatenate([-sin_t, -cos_t, -cos_t, -sin_t], 1)
    edge = np.zeros((P_SIZE, 256), np.float32)
    rows = np.stack([np.concatenate([t, edge], 0) for t in (from_u, from_v)])
    to_re = np.concatenate([cos_t, -sin_t], 0)
    to_im = np.concatenate([sin_t, cos_t], 0)
    blank = np.zeros_like(to_re)
    back_k = np.concatenate(
        [
            np.concatenate([to_re, blank, to_im, blank], 1),
            np.concatenate([blank, to_re, blank, to_im], 1),
        ],
        0,
    )
    weight = np.where(np.arange(half) == 0, 1.0, 2.0).astype(np.float32)
    one = np.concatenate([cos_t[:, :half] * weight, -sin_t[:, :half] * weight], 1)
    one[:, half] = cos_t[:, half]
    scale = SHARPNESS / P_SIZE**4
    back_l = np.kron(np.eye(GC, dtype=np.float32), one * np.float32(scale))
    bf = ml_dtypes.bfloat16
    return cols, rows, back_k.astype(bf), back_l.astype(bf)


def table_kernel(off_ref, edge_ref, cols_ref, rows_ref, m_ref, w_ref):
    bf16 = jnp.bfloat16
    lane = lax.broadcasted_iota(jnp.int32, cols_ref.shape, 1)
    line = lax.broadcasted_iota(jnp.int32, (WIN, 256), 0)
    for r in range(GR):
        if r == 0:
            inside_image = line >= jnp.where(edge_ref[0] == 1, HALF, 0)
        else:
            inside_image = line < jnp.where(edge_ref[1] == 1, WIN - HALF, WIN)
        for c in range(GC):
            i = r * GC + c
            row_at = off_ref[r, c, 0]
            start = c * P_SIZE - HALF + off_ref[r, c, 1]
            turn = jnp.where(start < 0, start + 256, start)
            turned = pltpu.roll(cols_ref[...], turn, 1)
            inside = (lane >= start) & (lane < start + P_SIZE)
            turned = jnp.where(inside, turned, 0.0)
            m_ref[r, c * 64 : (c + 1) * 64, :] = turned[:64].astype(bf16)
            m_ref[r, 256 + c * 16 : 256 + (c + 1) * 16, :] = jnp.concatenate([turned[64:]] * 2, 0).astype(bf16)
            for half in range(2):
                turned = pltpu.roll(rows_ref[half], row_at, 0)
                w_ref[i, half * WIN : (half + 1) * WIN, :] = jnp.where(inside_image, turned, 0.0).astype(bf16)


def patch_kernel(
    edge_ref, gap_ref, own_ref, prior_ref, far_ref, near_ref, pfar_ref, pnear_ref, m_ref, w_ref, back_k_ref, back_l_ref,
    out_ref, x_ref, z_ref, n_ref, y_ref, g_ref, max_ref, sum_ref, mom_ref,
):
    sections = own_ref.shape[0]
    stacked = sections + 2
    f32 = jnp.float32
    bf16 = jnp.bfloat16
    main = stacked * 32
    has_prior = jnp.where(edge_ref[2] == 1, 0.0, 1.0)

    odd = edge_ref[3] == 1

    def window(r, t):
        image = prior_ref.at[t] if t < 2 else own_ref.at[t - 2]
        near = pnear_ref[t] if t < 2 else near_ref[t - 2]
        far = pfar_ref[t] if t < 2 else far_ref[t - 2]
        if r == 0:
            return [jnp.where(odd, near, far), image[: WIN - HALF]]
        return [image[HALF:], jnp.where(odd, far, near)]

    sub = lax.broadcasted_iota(jnp.int32, (8, WIN), 0)
    for r in range(GR):
        nyquist = [[jnp.zeros((8, WIN), f32) for _ in range(3)] for _ in range(GC)]
        for pair in range(stacked // 2):
            both = jnp.concatenate(window(r, 2 * pair) + window(r, 2 * pair + 1), 0)
            first = lax.dot_general(m_ref[r], both, (((1,), (1,)), ((), ())), preferred_element_type=f32)
            if pair == 0:
                first = first * has_prior
            for c in range(GC):
                for k in range(2):
                    t = 2 * pair + k
                    for half in range(2):
                        x_ref[r * GC + c, t * 32 : (t + 1) * 32, half * WIN : (half + 1) * WIN] = first[
                            c * 64 + half * 32 : c * 64 + (half + 1) * 32, k * WIN : (k + 1) * WIN
                        ].astype(bf16)
                    block, at = (2, t) if t < 2 else ((t - 2) // 8, (t - 2) % 8)
                    row = first[256 + c * 16 : 264 + c * 16, k * WIN : (k + 1) * WIN]
                    nyquist[c][block] = jnp.where(sub == at, row, nyquist[c][block])
        for c in range(GC):
            i = r * GC + c
            x_ref[i, main : main + 16, :WIN] = jnp.concatenate(nyquist[c][:2], 0).astype(bf16)
            x_ref[i, main + 16 :, :WIN] = jnp.concatenate([nyquist[c][2]] * 2, 0).astype(bf16)
            x_ref[i, main:, WIN:] = jnp.zeros((32, WIN), bf16)

    for i in range(PATCHES):
        z_ref[i] = jnp.dot(x_ref[i], w_ref[i], preferred_element_type=f32).astype(bf16)

    def crossed(partner_p, partner_q, own_p, own_q):
        left = lax.broadcasted_iota(jnp.int32, partner_p.shape, 1) < 64
        twice_re = jnp.where(left, partner_p, partner_q)
        twice_im = jnp.where(left, partner_q, -partner_p)
        return twice_re * own_p + twice_im * own_q

    back = lax.broadcasted_iota(jnp.int32, (16, 128), 0)
    gap_rows = jnp.ones((16, 128), jnp.int32)
    for s in range(sections):
        gap_rows = jnp.where(back == s, gap_ref[s], gap_rows)
    even = back % 2 == 0
    for i in range(PATCHES):
        for s in range(sections):
            at = pl.multiple_of((s + 2 - gap_ref[s]) * 32, 32)
            row = i * 256 + (s // 2) * 32
            y_ref[row : row + 32, (s % 2) * 128 : (s % 2 + 1) * 128] = crossed(
                z_ref[i, pl.ds(at, 32), 0:128],
                z_ref[i, pl.ds(at, 32), 128:256],
                z_ref[i, (s + 2) * 32 : (s + 3) * 32, 0:128],
                z_ref[i, (s + 2) * 32 : (s + 3) * 32, 128:256],
            )
        own = z_ref[i, main : main + 16, :].astype(f32)
        n_ref[i, 8:24, :] = own
        n_ref[i, 0:8, :] = pltpu.roll(z_ref[i, main + 16 : main + 32, :].astype(f32)[0:8], 6, 0)
        one_up = n_ref[i, 7:23, :]
        two_up = n_ref[i, 6:22, :]
        partner_p = jnp.where(gap_rows == 1, one_up[:, :128], two_up[:, :128])
        partner_q = jnp.where(gap_rows == 1, one_up[:, 128:], two_up[:, 128:])
        line = crossed(partner_p, partner_q, own[:, :128], own[:, 128:])
        row = PATCHES * 256 + i * 16
        y_ref[row : row + 16, 0:128] = jnp.where(even, line, 0.0).astype(bf16)
        y_ref[row : row + 16, 128:256] = jnp.where(even, 0.0, line).astype(bf16)

    lines = jnp.dot(y_ref[PATCHES * 256 :, :], back_k_ref[:, :128], preferred_element_type=f32)
    first_row = lax.broadcasted_iota(jnp.int32, (32, 128), 0) == 0
    for i in range(PATCHES):
        mixed = jnp.dot(y_ref[i * 256 : (i + 1) * 256, :], back_k_ref[...], preferred_element_type=f32)
        at = (i % GC) * 64
        for pair in range(sections // 2):
            line = lines[i * 16 + 2 * pair : i * 16 + 2 * pair + 1] + lines[i * 16 + 2 * pair + 1 : i * 16 + 2 * pair + 2]
            part = slice(pair * 128, (pair + 1) * 128)
            g_ref[i // GC, at : at + 32, part] = mixed[pair * 32 : (pair + 1) * 32, 0:128].astype(bf16)
            g_ref[i // GC, at + 32 : at + 64, part] = jnp.where(
                first_row, line, mixed[pair * 32 : (pair + 1) * 32, 128:256]
            ).astype(bf16)

    signed = lax.broadcasted_iota(jnp.int32, (P_SIZE, 256), 0)
    signed = jnp.where(signed < HALF, signed, signed - P_SIZE).astype(f32)
    for r in range(GR):
        for block in range(sections * P_SIZE // 256):
            part = slice(block * 256, (block + 1) * 256)
            all_scores = jnp.dot(back_l_ref[...], g_ref[r, :, part], preferred_element_type=f32)
            for c in range(GC):
                i = r * GC + c
                scores = all_scores[c * 64 : (c + 1) * 64]
                top = jnp.max(scores, axis=0, keepdims=True)
                weights = jnp.exp(scores - top)
                max_ref[i : i + 1, part] = top
                sum_ref[i : i + 1, part] = jnp.sum(weights, axis=0, keepdims=True)
                mom_ref[i : i + 1, part] = jnp.sum(weights * signed, axis=0, keepdims=True)

    lane = lax.broadcasted_iota(jnp.int32, (PATCHES, 128), 1)
    left = lane < 64
    shift = lane % 64
    shift = jnp.where(shift < HALF, shift, shift - P_SIZE).astype(f32)
    place = lax.broadcasted_iota(jnp.int32, (PATCHES, sections), 1)
    rows_out = jnp.zeros((PATCHES, sections), f32)
    cols_out = jnp.zeros((PATCHES, sections), f32)
    for pair in range(sections // 2):
        part = slice(pair * 128, (pair + 1) * 128)
        top = max_ref[:, part]
        top_a = jnp.max(jnp.where(left, top, -jnp.inf), axis=1, keepdims=True)
        top_b = jnp.max(jnp.where(left, -jnp.inf, top), axis=1, keepdims=True)
        factor = jnp.exp(top - jnp.where(left, top_a, top_b))
        total = factor * sum_ref[:, part]
        moment = factor * mom_ref[:, part]
        for k in range(2):
            mine = left if k == 0 else jnp.logical_not(left)
            den = jnp.sum(jnp.where(mine, total, 0.0), axis=1, keepdims=True)
            along_u = jnp.sum(jnp.where(mine, total * shift, 0.0), axis=1, keepdims=True)
            along_v = jnp.sum(jnp.where(mine, moment, 0.0), axis=1, keepdims=True)
            here = place == 2 * pair + k
            rows_out = jnp.where(here, along_u / den / 8.0, rows_out)
            cols_out = jnp.where(here, along_v / den / 8.0, cols_out)
    out_ref[0:PATCHES, :] = rows_out
    out_ref[PATCHES:, :] = cols_out


def make_tables(offsets, edges):
    cols, rows, _, _ = make_constants()
    smem = pl.BlockSpec(memory_space=pltpu.SMEM)
    vmem = pl.BlockSpec(memory_space=pltpu.VMEM)
    bf16 = jnp.bfloat16
    return pl.pallas_call(
        table_kernel,
        out_shape=(
            jax.ShapeDtypeStruct((GR, 256 + GC * 16, 256), bf16),
            jax.ShapeDtypeStruct((PATCHES, 2 * WIN, 256), bf16),
        ),
        in_specs=[smem, smem, vmem, vmem],
        out_specs=(vmem, vmem),
        compiler_params=pltpu.CompilerParams(vmem_limit_bytes=16 * 1024 * 1024),
        cost_estimate=pl.CostEstimate(flops=4_000_000, bytes_accessed=4_000_000, transcendentals=0),
        name="make_tables",
    )(offsets, edges, cols, rows)


def measure(edges, gaps, images, prior, far, near, pfar, pnear, m_table, w_table):
    sections = images.shape[0]
    rows_x = (sections + 2) * 32 + 32
    _, _, back_k, back_l = make_constants()
    smem = pl.BlockSpec(memory_space=pltpu.SMEM)
    vmem = pl.BlockSpec(memory_space=pltpu.VMEM)
    bf16 = jnp.bfloat16
    f32 = jnp.float32
    return pl.pallas_call(
        patch_kernel,
        out_shape=jax.ShapeDtypeStruct((2 * PATCHES, sections), f32),
        in_specs=[smem, smem] + [vmem] * 10,
        out_specs=vmem,
        scratch_shapes=[
            pltpu.VMEM((PATCHES, rows_x, 2 * WIN), bf16),
            pltpu.VMEM((PATCHES, rows_x, 256), bf16),
            pltpu.VMEM((PATCHES, 24, 256), f32),
            pltpu.VMEM((PATCHES * (sections * 16 + 16), 256), bf16),
            pltpu.VMEM((GR, 256, sections * 64), bf16),
            pltpu.VMEM((PATCHES, sections * 64), f32),
            pltpu.VMEM((PATCHES, sections * 64), f32),
            pltpu.VMEM((PATCHES, sections * 64), f32),
        ],
        compiler_params=pltpu.CompilerParams(vmem_limit_bytes=32 * 1024 * 1024),
        cost_estimate=pl.CostEstimate(flops=2_000_000_000, bytes_accessed=6_000_000, transcendentals=600_000),
        name="measure",
    )(edges, gaps, images, prior, far, near, pfar, pnear, m_table, w_table, back_k, back_l)


def relaxed_step(extended):
    middle = extended[:, 1:-1]
    widened = jnp.pad(middle, ((0, 0), (0, 0), (1, 1), (0, 0)))
    beside = extended[:, :-2] + extended[:, 2:] + widened[:, :, :-2] + widened[:, :, 2:]
    return 0.5 * middle + 0.125 * beside


def earlier_groups(total):
    place = lax.axis_index("gz")
    count = lax.axis_size("gz")
    other = lax.ppermute(total, "gz", [(i, i ^ 1) for i in range(count)])
    pair = total + other
    across = lax.ppermute(pair, "gz", [(i, (i + 2) % count) for i in range(count)])
    return jnp.where(place >= 2, across, 0.0) + jnp.where(place % 2 == 1, other, 0.0)


def exchange_edges(value, odd):
    rows = value.shape[1]
    top, bottom = value[:, :HALF], value[:, rows - HALF :]
    far = swap_far(jnp.where(odd, bottom, top))
    near = swap_near(jnp.where(odd, top, bottom))
    return near, far


def local(images, offsets, gaps):
    sections = images.shape[0]
    place = lax.axis_index("xy")
    last = lax.axis_size("xy") - 1
    odd = place % 2 == 1
    even = jnp.logical_not(odd)
    edges = jnp.stack([place == 0, place == last, lax.axis_index("gz") == 0, odd]).astype(jnp.int32)
    m_table, w_table = make_tables(offsets, edges)
    prior = ring(images[sections - 2 :], "gz", 1)
    near, far = exchange_edges(images, odd)
    pnear, pfar = exchange_edges(prior, odd)
    measured = measure(edges, gaps, images, prior, far, near, pfar, pnear, m_table, w_table)
    far = swap_far(measured)
    near = swap_near(measured)
    above = jnp.where(place == 0, 0.0, jnp.where(even, far, near)).reshape(2, GR, GC, sections)
    below = jnp.where(place == last, 0.0, jnp.where(even, near, far)).reshape(2, GR, GC, sections)
    measured = measured.reshape(2, GR, GC, sections)
    wide = relaxed_step(jnp.concatenate([above, measured, below], 1))
    row = place * GR + jnp.arange(-1, GR + 1)
    inside = (row >= 0) & (row < GR * (last + 1))
    wide = jnp.where(inside[None, :, None, None], wide, 0.0)
    smoothed = relaxed_step(wide)
    earlier_sum = earlier_groups(jnp.sum(smoothed, axis=3))
    triangle = jnp.triu(jnp.ones((sections, sections), jnp.float32))
    running = jnp.dot(smoothed.reshape(2 * PATCHES, sections), triangle, precision=lax.Precision.HIGHEST)
    composed = running.reshape(smoothed.shape) + earlier_sum[..., None]
    return smoothed.transpose(0, 3, 1, 2), composed.transpose(0, 3, 1, 2)


def solution(mesh):
    in_specs = (P("gz", "xy", None), P("xy", None, None), P("gz"))
    out_specs = (P(None, "gz", "xy", None), P(None, "gz", "xy", None))
    return jax.shard_map(local, mesh=mesh, in_specs=in_specs, out_specs=out_specs, check_vma=False)
```

```python
import math

import jax
import jax.numpy as jnp
import ml_dtypes
import numpy as np
from jax import lax
from jax.experimental import pallas as pl
from jax.experimental.pallas import tpu as pltpu
from jax.sharding import PartitionSpec as P

P_SIZE = 64
HALF = 32
SHARPNESS = 16.0
WIN = 128
GR = 2
GC = 4
PATCHES = GR * GC
AT_TOP, AT_BOTTOM, FIRST_GROUP, ODD, GAPS, OFFSETS = 0, 1, 2, 3, 4, 20


def ring(value, axis, steps):
    count = lax.axis_size(axis)
    return lax.ppermute(value, axis, [(source, (source + steps) % count) for source in range(count)])


def swap_near(value):
    count = lax.axis_size("xy")
    return lax.ppermute(value, "xy", [(i, i ^ 1) for i in range(count)])


def swap_far(value):
    count = lax.axis_size("xy")
    return lax.ppermute(value, "xy", [(i, (i + 1 if i % 2 else i - 1) % count) for i in range(count)])


def tables():
    indices = np.arange(P_SIZE)
    angles = (indices[:, None] * indices[None, :] % P_SIZE) * (2.0 * math.pi / P_SIZE)
    cos_t = np.cos(angles).astype(np.float32).astype(ml_dtypes.bfloat16).astype(np.float32)
    sin_t = np.sin(angles).astype(np.float32).astype(ml_dtypes.bfloat16).astype(np.float32)
    sin_t = np.where(np.abs(sin_t) < 1e-6, np.float32(0), sin_t)
    return cos_t, sin_t


def make_constants():
    cos_t, sin_t = tables()
    half = P_SIZE // 2
    cols = np.zeros((P_SIZE + 8, 256), np.float32)
    cols[:half, :P_SIZE] = cos_t[:half]
    cols[half:P_SIZE, :P_SIZE] = sin_t[:half]
    cols[P_SIZE:, :P_SIZE] = cos_t[half]
    from_u = np.concatenate([cos_t, -sin_t, -sin_t, cos_t], 1)
    from_v = np.concatenate([-sin_t, -cos_t, -cos_t, -sin_t], 1)
    edge = np.zeros((P_SIZE, 256), np.float32)
    rows = np.stack([np.concatenate([t, edge], 0) for t in (from_u, from_v)])
    to_re = np.concatenate([cos_t, -sin_t], 0)
    to_im = np.concatenate([sin_t, cos_t], 0)
    blank = np.zeros_like(to_re)
    back_k = np.concatenate(
        [
            np.concatenate([to_re, blank, to_im, blank], 1),
            np.concatenate([blank, to_re, blank, to_im], 1),
        ],
        0,
    )
    weight = np.where(np.arange(half) == 0, 1.0, 2.0).astype(np.float32)
    one = np.concatenate([cos_t[:, :half] * weight, -sin_t[:, :half] * weight], 1)
    one[:, half] = cos_t[:, half]
    scale = SHARPNESS / P_SIZE**4
    back_l = np.kron(np.eye(GC, dtype=np.float32), one * np.float32(scale))
    bf = ml_dtypes.bfloat16
    return cols, rows, back_k.astype(bf), back_l.astype(bf)


def table_kernel(scalar_ref, cols_ref, rows_ref, m_ref, w_ref):
    bf16 = jnp.bfloat16
    lane = lax.broadcasted_iota(jnp.int32, cols_ref.shape, 1)
    line = lax.broadcasted_iota(jnp.int32, (WIN, 256), 0)
    for r in range(GR):
        if r == 0:
            inside_image = line >= jnp.where(scalar_ref[AT_TOP] == 1, HALF, 0)
        else:
            inside_image = line < jnp.where(scalar_ref[AT_BOTTOM] == 1, WIN - HALF, WIN)
        for c in range(GC):
            i = r * GC + c
            row_at = scalar_ref[OFFSETS + 2 * i]
            start = c * P_SIZE - HALF + scalar_ref[OFFSETS + 2 * i + 1]
            turn = jnp.where(start < 0, start + 256, start)
            turned = pltpu.roll(cols_ref[...], turn, 1)
            inside = (lane >= start) & (lane < start + P_SIZE)
            turned = jnp.where(inside, turned, 0.0)
            m_ref[r, c * 64 : (c + 1) * 64, :] = turned[:64].astype(bf16)
            m_ref[r, 256 + c * 16 : 256 + (c + 1) * 16, :] = jnp.concatenate([turned[64:]] * 2, 0).astype(bf16)
            for half in range(2):
                turned = pltpu.roll(rows_ref[half], row_at, 0)
                w_ref[i, half * WIN : (half + 1) * WIN, :] = jnp.where(inside_image, turned, 0.0).astype(bf16)


def transform_pair(r, pair, both, m_ref, x_ref, nyquist, scale=None):
    f32 = jnp.float32
    sub = lax.broadcasted_iota(jnp.int32, (8, WIN), 0)
    first = lax.dot_general(m_ref[r], both, (((1,), (1,)), ((), ())), preferred_element_type=f32)
    if scale is not None:
        first = first * scale
    for c in range(GC):
        for k in range(2):
            t = 2 * pair + k
            for half in range(2):
                x_ref[r * GC + c, t * 32 : (t + 1) * 32, half * WIN : (half + 1) * WIN] = first[
                    c * 64 + half * 32 : c * 64 + (half + 1) * 32, k * WIN : (k + 1) * WIN
                ].astype(jnp.bfloat16)
            row = first[256 + c * 16 : 264 + c * 16, k * WIN : (k + 1) * WIN]
            nyquist[c][t // 8] = jnp.where(sub == t % 8, row, nyquist[c][t // 8])


def store_nyquist(r, main, x_ref, nyquist):
    bf16 = jnp.bfloat16
    for c in range(GC):
        i = r * GC + c
        x_ref[i, main : main + 16, :WIN] = jnp.concatenate(nyquist[c], 0).astype(bf16)
        x_ref[i, main : main + 16, WIN:] = jnp.zeros((16, WIN), bf16)


def crossed(partner_p, partner_q, own_p, own_q):
    left = lax.broadcasted_iota(jnp.int32, partner_p.shape, 1) < 64
    twice_re = jnp.where(left, partner_p, partner_q)
    twice_im = jnp.where(left, partner_q, -partner_p)
    return twice_re * own_p + twice_im * own_q


def gap_column(scalar_ref):
    row = lax.broadcasted_iota(jnp.int32, (16, 128), 0)
    gaps = jnp.ones((16, 128), jnp.int32)
    for s in range(16):
        gaps = jnp.where(row == s, scalar_ref[GAPS + s], gaps)
    return gaps


def cross_nyquist(i, own, prior, gaps, n_ref, y_ref, row):
    even = lax.broadcasted_iota(jnp.int32, (16, 128), 0) % 2 == 0
    n_ref[i, 8:24, :] = own
    n_ref[i, 0:8, :] = prior
    one_up = n_ref[i, 7:23, :]
    two_up = n_ref[i, 6:22, :]
    partner_p = jnp.where(gaps == 1, one_up[:, :128], two_up[:, :128])
    partner_q = jnp.where(gaps == 1, one_up[:, 128:], two_up[:, 128:])
    line = crossed(partner_p, partner_q, own[:, :128], own[:, 128:])
    y_ref[row : row + 16, 0:128] = jnp.where(even, line, 0.0).astype(jnp.bfloat16)
    y_ref[row : row + 16, 128:256] = jnp.where(even, 0.0, line).astype(jnp.bfloat16)


def correlate_pairs(pairs, first, y_ref, g_ref, back_k_ref, back_l_ref, max_ref, sum_ref, mom_ref):
    f32 = jnp.float32
    bf16 = jnp.bfloat16
    lines = jnp.dot(y_ref[PATCHES * pairs * 32 :, :], back_k_ref[:, :128], preferred_element_type=f32)
    first_row = lax.broadcasted_iota(jnp.int32, (32, 128), 0) == 0
    for i in range(PATCHES):
        mixed = jnp.dot(y_ref[i * pairs * 32 : (i + 1) * pairs * 32, :], back_k_ref[...], preferred_element_type=f32)
        at = (i % GC) * 64
        for pair in range(pairs):
            row = i * 16 + first + 2 * pair
            line = lines[row : row + 1] + lines[row + 1 : row + 2]
            part = slice(pair * 128, (pair + 1) * 128)
            g_ref[i // GC, at : at + 32, part] = mixed[pair * 32 : (pair + 1) * 32, 0:128].astype(bf16)
            g_ref[i // GC, at + 32 : at + 64, part] = jnp.where(
                first_row, line, mixed[pair * 32 : (pair + 1) * 32, 128:256]
            ).astype(bf16)
    for r in range(GR):
        for lane_at in range(0, pairs * 128, 256):
            part = slice(lane_at, min(lane_at + 256, pairs * 128))
            all_scores = jnp.dot(back_l_ref[...], g_ref[r, :, part], preferred_element_type=f32)
            signed = lax.broadcasted_iota(jnp.int32, (P_SIZE, all_scores.shape[1]), 0)
            signed = jnp.where(signed < HALF, signed, signed - P_SIZE).astype(f32)
            for c in range(GC):
                i = r * GC + c
                scores = all_scores[c * 64 : (c + 1) * 64]
                top = jnp.max(scores, axis=0, keepdims=True)
                weights = jnp.exp(scores - top)
                max_ref[i : i + 1, part] = top
                sum_ref[i : i + 1, part] = jnp.sum(weights, axis=0, keepdims=True)
                mom_ref[i : i + 1, part] = jnp.sum(weights * signed, axis=0, keepdims=True)


def merge_pairs(pairs, first, rows_out, cols_out, max_ref, sum_ref, mom_ref):
    f32 = jnp.float32
    lane = lax.broadcasted_iota(jnp.int32, (PATCHES, 128), 1)
    left = lane < 64
    shift = lane % 64
    shift = jnp.where(shift < HALF, shift, shift - P_SIZE).astype(f32)
    place = lax.broadcasted_iota(jnp.int32, rows_out.shape, 1)
    for pair in range(pairs):
        part = slice(pair * 128, (pair + 1) * 128)
        top = max_ref[:, part]
        top_a = jnp.max(jnp.where(left, top, -jnp.inf), axis=1, keepdims=True)
        top_b = jnp.max(jnp.where(left, -jnp.inf, top), axis=1, keepdims=True)
        factor = jnp.exp(top - jnp.where(left, top_a, top_b))
        total = factor * sum_ref[:, part]
        moment = factor * mom_ref[:, part]
        for k in range(2):
            mine = left if k == 0 else jnp.logical_not(left)
            den = jnp.sum(jnp.where(mine, total, 0.0), axis=1, keepdims=True)
            along_u = jnp.sum(jnp.where(mine, total * shift, 0.0), axis=1, keepdims=True)
            along_v = jnp.sum(jnp.where(mine, moment, 0.0), axis=1, keepdims=True)
            here = place == first + 2 * pair + k
            rows_out = jnp.where(here, along_u / den / 8.0, rows_out)
            cols_out = jnp.where(here, along_v / den / 8.0, cols_out)
    return rows_out, cols_out


def own_kernel(
    scalar_ref, own_ref, far_ref, near_ref, m_ref, w_ref, back_k_ref, back_l_ref,
    out_ref, head_ref, x_ref, z_ref, n_ref, y_ref, g_ref, max_ref, sum_ref, mom_ref,
):
    sections = own_ref.shape[0]
    pairs = sections // 2 - 1
    f32 = jnp.float32
    main = sections * 32
    odd = scalar_ref[ODD] == 1

    def window(r, t):
        if r == 0:
            return [jnp.where(odd, near_ref[t], far_ref[t]), own_ref[t, : WIN - HALF]]
        return [own_ref[t, HALF:], jnp.where(odd, far_ref[t], near_ref[t])]

    for r in range(GR):
        nyquist = [[jnp.zeros((8, WIN), f32) for _ in range(2)] for _ in range(GC)]
        for pair in range(sections // 2):
            both = jnp.concatenate(window(r, 2 * pair) + window(r, 2 * pair + 1), 0)
            transform_pair(r, pair, both, m_ref, x_ref, nyquist)
        store_nyquist(r, main, x_ref, nyquist)

    for i in range(PATCHES):
        spectrum = jnp.dot(x_ref[i], w_ref[i], preferred_element_type=f32).astype(jnp.bfloat16)
        z_ref[i] = spectrum
        head_ref[i, 0:64, :] = spectrum[0:64]
        head_ref[i, 64:80, :] = spectrum[main : main + 16]

    gaps = gap_column(scalar_ref)
    for i in range(PATCHES):
        for s in range(2, sections):
            at = pl.multiple_of((s - scalar_ref[GAPS + s]) * 32, 32)
            row = (i * pairs + s // 2 - 1) * 32
            y_ref[row : row + 32, (s % 2) * 128 : (s % 2 + 1) * 128] = crossed(
                z_ref[i, pl.ds(at, 32), 0:128],
                z_ref[i, pl.ds(at, 32), 128:256],
                z_ref[i, s * 32 : (s + 1) * 32, 0:128],
                z_ref[i, s * 32 : (s + 1) * 32, 128:256],
            )
        own = z_ref[i, main : main + 16, :].astype(f32)
        cross_nyquist(i, own, jnp.zeros((8, 256), f32), gaps, n_ref, y_ref, PATCHES * pairs * 32 + i * 16)

    correlate_pairs(pairs, 2, y_ref, g_ref, back_k_ref, back_l_ref, max_ref, sum_ref, mom_ref)
    zeros = jnp.zeros((PATCHES, sections), f32)
    rows_out, cols_out = merge_pairs(pairs, 2, zeros, zeros, max_ref, sum_ref, mom_ref)
    out_ref[0:PATCHES, :] = rows_out
    out_ref[PATCHES:, :] = cols_out


def head_kernel(
    scalar_ref, prior_ref, head_ref, part_ref, m_ref, w_ref, back_k_ref, back_l_ref,
    out_ref, x_ref, z_ref, n_ref, y_ref, g_ref, max_ref, sum_ref, mom_ref,
):
    f32 = jnp.float32
    has_prior = jnp.where(scalar_ref[FIRST_GROUP] == 1, 0.0, 1.0)
    for r in range(GR):
        nyquist = [[jnp.zeros((8, WIN), f32) for _ in range(2)] for _ in range(GC)]
        at = 0 if r == 0 else HALF
        both = jnp.concatenate([prior_ref[0, at : at + WIN], prior_ref[1, at : at + WIN]], 0)
        transform_pair(r, 0, both, m_ref, x_ref, nyquist, has_prior)
        store_nyquist(r, 64, x_ref, nyquist)

    gaps = gap_column(scalar_ref)
    for i in range(PATCHES):
        spectrum = jnp.dot(x_ref[i], w_ref[i], preferred_element_type=f32)
        z_ref[i, 0:64, :] = spectrum[0:64].astype(jnp.bfloat16)
        z_ref[i, 64:128, :] = head_ref[i, 0:64, :]
        for s in range(2):
            at = pl.multiple_of((s + 2 - scalar_ref[GAPS + s]) * 32, 32)
            y_ref[i * 32 : (i + 1) * 32, s * 128 : (s + 1) * 128] = crossed(
                z_ref[i, pl.ds(at, 32), 0:128],
                z_ref[i, pl.ds(at, 32), 128:256],
                head_ref[i, s * 32 : (s + 1) * 32, 0:128],
                head_ref[i, s * 32 : (s + 1) * 32, 128:256],
            )
        prior = pltpu.roll(spectrum[64:72].astype(jnp.bfloat16).astype(f32), 6, 0)
        cross_nyquist(i, head_ref[i, 64:80, :].astype(f32), prior, gaps, n_ref, y_ref, PATCHES * 32 + i * 16)

    correlate_pairs(1, 0, y_ref, g_ref, back_k_ref, back_l_ref, max_ref, sum_ref, mom_ref)
    rows_out, cols_out = merge_pairs(1, 0, part_ref[0:PATCHES, :], part_ref[PATCHES:, :], max_ref, sum_ref, mom_ref)
    out_ref[0:PATCHES, :] = rows_out
    out_ref[PATCHES:, :] = cols_out


def call(kernel, name, out_shape, scratch, operands, flops, limit):
    smem = pl.BlockSpec(memory_space=pltpu.SMEM)
    vmem = pl.BlockSpec(memory_space=pltpu.VMEM)
    return pl.pallas_call(
        kernel,
        out_shape=out_shape,
        in_specs=[smem] + [vmem] * (len(operands) - 1),
        out_specs=tuple(vmem for _ in out_shape),
        scratch_shapes=scratch,
        compiler_params=pltpu.CompilerParams(vmem_limit_bytes=limit * 1024 * 1024),
        cost_estimate=pl.CostEstimate(flops=flops, bytes_accessed=4_000_000, transcendentals=0),
        name=name,
    )(*operands)


def work_buffers(sections, rows_x, rows_z, pairs):
    bf16 = jnp.bfloat16
    return [
        pltpu.VMEM((PATCHES, rows_x, 2 * WIN), bf16),
        pltpu.VMEM((PATCHES, rows_z, 256), bf16),
        pltpu.VMEM((PATCHES, 24, 256), jnp.float32),
        pltpu.VMEM((PATCHES * (pairs * 32 + 16), 256), bf16),
        pltpu.VMEM((GR, 256, pairs * 128), bf16),
    ] + [pltpu.VMEM((PATCHES, pairs * 128), jnp.float32)] * 3


def make_tables(scalars):
    cols, rows, _, _ = make_constants()
    bf16 = jnp.bfloat16
    shapes = (
        jax.ShapeDtypeStruct((GR, 256 + GC * 16, 256), bf16),
        jax.ShapeDtypeStruct((PATCHES, 2 * WIN, 256), bf16),
    )
    return call(table_kernel, "make_tables", shapes, [], (scalars, cols, rows), 4_000_000, 16)


def measure_own(scalars, images, far, near, m_table, w_table):
    sections = images.shape[0]
    _, _, back_k, back_l = make_constants()
    rows_x = sections * 32 + 16
    shapes = (
        jax.ShapeDtypeStruct((2 * PATCHES, sections), jnp.float32),
        jax.ShapeDtypeStruct((PATCHES, 80, 256), jnp.bfloat16),
    )
    scratch = work_buffers(sections, rows_x, rows_x, sections // 2 - 1)
    operands = (scalars, images, far, near, m_table, w_table, back_k, back_l)
    return call(own_kernel, "measure_own", shapes, scratch, operands, 3_000_000_000, 32)


def measure_head(scalars, prior, head, part, m_table, w_table):
    _, _, back_k, back_l = make_constants()
    shapes = (jax.ShapeDtypeStruct(part.shape, jnp.float32),)
    scratch = work_buffers(part.shape[1], 80, 128, 1)
    operands = (scalars, prior, head, part, m_table, w_table, back_k, back_l)
    return call(head_kernel, "measure_head", shapes, scratch, operands, 500_000_000, 16)[0]


def relaxed_step(extended):
    middle = extended[:, 1:-1]
    widened = jnp.pad(middle, ((0, 0), (0, 0), (1, 1), (0, 0)))
    beside = extended[:, :-2] + extended[:, 2:] + widened[:, :, :-2] + widened[:, :, 2:]
    return 0.5 * middle + 0.125 * beside


def earlier_groups(total):
    place = lax.axis_index("gz")
    count = lax.axis_size("gz")
    other = lax.ppermute(total, "gz", [(i, i ^ 1) for i in range(count)])
    pair = total + other
    across = lax.ppermute(pair, "gz", [(i, (i + 2) % count) for i in range(count)])
    return jnp.where(place >= 2, across, 0.0) + jnp.where(place % 2 == 1, other, 0.0)


def local(images, offsets, gaps):
    sections = images.shape[0]
    rows = images.shape[1]
    place = lax.axis_index("xy")
    last = lax.axis_size("xy") - 1
    odd = place % 2 == 1
    even = jnp.logical_not(odd)
    flags = jnp.stack([place == 0, place == last, lax.axis_index("gz") == 0, odd]).astype(jnp.int32)
    scalars = jnp.concatenate([flags, gaps, offsets.reshape(-1)])
    m_table, w_table = make_tables(scalars)
    top, bottom = images[:, :HALF], images[:, rows - HALF :]
    far = swap_far(jnp.where(odd, bottom, top))
    near = swap_near(jnp.where(odd, top, bottom))
    tail = slice(sections - 2, sections)
    low = jnp.where(even, far[tail], near[tail])
    high = jnp.where(even, near[tail], far[tail])
    kept = HALF + 16
    windows = jnp.concatenate([low, images[tail, :kept], images[tail, rows - kept :], high], axis=1)
    prior = ring(windows, "gz", 1)
    part, head = measure_own(scalars, images, far, near, m_table, w_table)
    measured = measure_head(scalars, prior, head, part, m_table, w_table)
    near = swap_near(measured)
    far = swap_far(measured)
    above = jnp.where(place == 0, 0.0, jnp.where(odd, near, far)).reshape(2, GR, GC, sections)
    below = jnp.where(place == last, 0.0, jnp.where(odd, far, near)).reshape(2, GR, GC, sections)
    measured = measured.reshape(2, GR, GC, sections)
    wide = relaxed_step(jnp.concatenate([above, measured, below], 1))
    row = place * GR + jnp.arange(-1, GR + 1)
    inside = (row >= 0) & (row < GR * (last + 1))
    wide = jnp.where(inside[None, :, None, None], wide, 0.0)
    smoothed = relaxed_step(wide)
    earlier_sum = earlier_groups(jnp.sum(smoothed, axis=3))
    triangle = jnp.triu(jnp.ones((sections, sections), jnp.float32))
    running = jnp.dot(smoothed.reshape(2 * PATCHES, sections), triangle, precision=lax.Precision.HIGHEST)
    running = lax.optimization_barrier(running)
    composed = running.reshape(smoothed.shape) + earlier_sum[..., None]
    return smoothed.transpose(0, 3, 1, 2), composed.transpose(0, 3, 1, 2)


def solution(mesh):
    in_specs = (P("gz", "xy", None), P("xy", None, None), P("gz"))
    out_specs = (P(None, "gz", "xy", None), P(None, "gz", "xy", None))
    return jax.shard_map(local, mesh=mesh, in_specs=in_specs, out_specs=out_specs, check_vma=False)
```

```python
from functools import partial
import math

import jax
import jax.numpy as jnp
import ml_dtypes
import numpy as np
from jax import lax
from jax.experimental import pallas as pl
from jax.experimental.pallas import tpu as pltpu
from jax.sharding import PartitionSpec as P

P_SIZE = 64
HALF = 32
SHARPNESS = 16.0
WIN = 128
GR = 2
GC = 4
PATCHES = GR * GC
AT_TOP, AT_BOTTOM, FIRST_GROUP, ODD, GAPS, OFFSETS = 0, 1, 2, 3, 4, 20


def ring(value, axis, steps):
    count = lax.axis_size(axis)
    return lax.ppermute(value, axis, [(source, (source + steps) % count) for source in range(count)])


def swap_near(value):
    count = lax.axis_size("xy")
    return lax.ppermute(value, "xy", [(i, i ^ 1) for i in range(count)])


def swap_far(value):
    count = lax.axis_size("xy")
    return lax.ppermute(value, "xy", [(i, (i + 1 if i % 2 else i - 1) % count) for i in range(count)])


def tables():
    indices = np.arange(P_SIZE)
    angles = (indices[:, None] * indices[None, :] % P_SIZE) * (2.0 * math.pi / P_SIZE)
    cos_t = np.cos(angles).astype(np.float32).astype(ml_dtypes.bfloat16).astype(np.float32)
    sin_t = np.sin(angles).astype(np.float32).astype(ml_dtypes.bfloat16).astype(np.float32)
    sin_t = np.where(np.abs(sin_t) < 1e-6, np.float32(0), sin_t)
    return cos_t, sin_t


def make_constants():
    cos_t, sin_t = tables()
    half = P_SIZE // 2
    cols = np.zeros((P_SIZE + 8, 256), np.float32)
    cols[:half, :P_SIZE] = cos_t[:half]
    cols[half:P_SIZE, :P_SIZE] = sin_t[:half]
    cols[P_SIZE:, :P_SIZE] = cos_t[half]
    rows = np.zeros((WIN, 2 * P_SIZE), np.float32)
    rows[:P_SIZE] = np.concatenate([cos_t, -sin_t], 1)
    to_re = np.concatenate([cos_t, -sin_t], 0)
    to_im = np.concatenate([sin_t, cos_t], 0)
    blank = np.zeros_like(to_re)
    back_k = np.concatenate(
        [
            np.concatenate([to_re, blank, to_im, blank], 1),
            np.concatenate([blank, to_re, blank, to_im], 1),
        ],
        0,
    )
    weight = np.where(np.arange(half) == 0, 1.0, 2.0).astype(np.float32)
    one = np.concatenate([cos_t[:, :half] * weight, -sin_t[:, :half] * weight], 1)
    one[:, half] = cos_t[:, half]
    scale = SHARPNESS / P_SIZE**4
    back_l = np.kron(np.eye(GC, dtype=np.float32), one * np.float32(scale))
    bf = ml_dtypes.bfloat16
    return cols, rows, back_k.astype(bf), back_l.astype(bf)


def table_kernel(scalar_ref, cols_ref, rows_ref, m_ref, w_ref):
    bf16 = jnp.bfloat16
    lane = lax.broadcasted_iota(jnp.int32, cols_ref.shape, 1)
    line = lax.broadcasted_iota(jnp.int32, (WIN, 128), 0)
    sign = jnp.where(lax.broadcasted_iota(jnp.int32, (WIN, 128), 1) < P_SIZE, 1.0, -1.0)
    for r in range(GR):
        inside_image = line >= jnp.where(scalar_ref[AT_TOP if r == 0 else AT_BOTTOM] == 1, HALF, 0)
        for c in range(GC):
            i = r * GC + c
            row_at = scalar_ref[OFFSETS + 2 * i] + r * HALF
            start = c * P_SIZE - HALF + scalar_ref[OFFSETS + 2 * i + 1]
            turn = jnp.where(start < 0, start + 256, start)
            turned = pltpu.roll(cols_ref[...], turn, 1)
            inside = (lane >= start) & (lane < start + P_SIZE)
            turned = jnp.where(inside, turned, 0.0)
            m_ref[r, c * 64 : (c + 1) * 64, :] = turned[:64].astype(bf16)
            m_ref[r, 256 + c * 16 : 256 + (c + 1) * 16, :] = jnp.concatenate([turned[64:]] * 2, 0).astype(bf16)
            straight = jnp.where(inside_image, pltpu.roll(rows_ref[...], row_at, 0), 0.0)
            crossed_over = pltpu.roll(straight, P_SIZE, 1)
            w_ref[i, 0:WIN, 0:128] = straight.astype(bf16)
            w_ref[i, 0:WIN, 128:256] = crossed_over.astype(bf16)
            w_ref[i, WIN:, 0:128] = (crossed_over * sign).astype(bf16)
            w_ref[i, WIN:, 128:256] = (straight * -sign).astype(bf16)


def crossed(partner_p, partner_q, own_p, own_q):
    left = lax.broadcasted_iota(jnp.int32, partner_p.shape, 1) < 64
    twice_re = jnp.where(left, partner_p, partner_q)
    twice_im = jnp.where(left, partner_q, -partner_p)
    return twice_re * own_p + twice_im * own_q


def gap_column(scalar_ref):
    row = lax.broadcasted_iota(jnp.int32, (16, 128), 0)
    gaps = jnp.ones((16, 128), jnp.int32)
    for s in range(16):
        gaps = jnp.where(row == s, scalar_ref[GAPS + s], gaps)
    return gaps


def cross_nyquist(i, own, prior, gaps, n_ref, y_ref, row):
    even = lax.broadcasted_iota(jnp.int32, (16, 128), 0) % 2 == 0
    n_ref[i, 8:24, :] = own
    n_ref[i, 0:8, :] = prior
    one_up = n_ref[i, 7:23, :]
    two_up = n_ref[i, 6:22, :]
    partner_p = jnp.where(gaps == 1, one_up[:, :128], two_up[:, :128])
    partner_q = jnp.where(gaps == 1, one_up[:, 128:], two_up[:, 128:])
    line = crossed(partner_p, partner_q, own[:, :128], own[:, 128:])
    y_ref[row : row + 16, 0:128] = jnp.where(even, line, 0.0).astype(jnp.bfloat16)
    y_ref[row : row + 16, 128:256] = jnp.where(even, 0.0, line).astype(jnp.bfloat16)


def row_kernel(
    is_far, scalar_ref, own_ref, halo_ref, prior_ref, phalo_ref, m_ref, w_ref, back_k_ref, back_l_ref, *rest
):
    if is_far:
        part_ref, *rest = rest
    out_ref, x_ref, z_ref, n_ref, y_ref, g_ref, max_ref, sum_ref, mom_ref = rest
    sections = own_ref.shape[0]
    stacked = sections + 2
    pairs = sections // 2
    f32 = jnp.float32
    bf16 = jnp.bfloat16
    main = stacked * 32
    r = scalar_ref[ODD] if is_far else 1 - scalar_ref[ODD]
    own_at = pl.multiple_of(r * HALF, HALF)
    has_prior = jnp.where(scalar_ref[FIRST_GROUP] == 1, 0.0, 1.0)

    def window(t):
        if t < 2:
            return [phalo_ref[t], prior_ref[t, pl.ds(own_at, WIN - HALF), :]]
        return [halo_ref[t - 2], own_ref[t - 2, pl.ds(own_at, WIN - HALF), :]]

    sub = lax.broadcasted_iota(jnp.int32, (8, WIN), 0)
    nyquist = [[jnp.zeros((8, WIN), f32) for _ in range(3)] for _ in range(GC)]
    for pair in range(stacked // 2):
        both = jnp.concatenate(window(2 * pair) + window(2 * pair + 1), 0)
        first = lax.dot_general(m_ref[r], both, (((1,), (1,)), ((), ())), preferred_element_type=f32)
        if pair == 0:
            first = first * has_prior
        for c in range(GC):
            for k in range(2):
                t = 2 * pair + k
                for half in range(2):
                    x_ref[c, t * 32 : (t + 1) * 32, half * WIN : (half + 1) * WIN] = first[
                        c * 64 + half * 32 : c * 64 + (half + 1) * 32, k * WIN : (k + 1) * WIN
                    ].astype(bf16)
                block, at = (2, t) if t < 2 else ((t - 2) // 8, (t - 2) % 8)
                line = first[256 + c * 16 : 264 + c * 16, k * WIN : (k + 1) * WIN]
                nyquist[c][block] = jnp.where(sub == at, line, nyquist[c][block])
    for c in range(GC):
        x_ref[c, main : main + 16, :WIN] = jnp.concatenate(nyquist[c][:2], 0).astype(bf16)
        x_ref[c, main + 16 :, :WIN] = jnp.concatenate([nyquist[c][2]] * 2, 0).astype(bf16)
        x_ref[c, main:, WIN:] = jnp.zeros((32, WIN), bf16)

    for c in range(GC):
        z_ref[c] = jnp.dot(x_ref[c], w_ref[r * GC + c], preferred_element_type=f32).astype(bf16)

    gaps = gap_column(scalar_ref)
    for c in range(GC):
        for s in range(sections):
            at = pl.multiple_of((s + 2 - scalar_ref[GAPS + s]) * 32, 32)
            row = (c * pairs + s // 2) * 32
            y_ref[row : row + 32, (s % 2) * 128 : (s % 2 + 1) * 128] = crossed(
                z_ref[c, pl.ds(at, 32), 0:128],
                z_ref[c, pl.ds(at, 32), 128:256],
                z_ref[c, (s + 2) * 32 : (s + 3) * 32, 0:128],
                z_ref[c, (s + 2) * 32 : (s + 3) * 32, 128:256],
            )
        own = z_ref[c, main : main + 16, :].astype(f32)
        prior = pltpu.roll(z_ref[c, main + 16 : main + 32, :].astype(f32)[0:8], 6, 0)
        cross_nyquist(c, own, prior, gaps, n_ref, y_ref, GC * pairs * 32 + c * 16)

    lines = jnp.dot(y_ref[GC * pairs * 32 :, :], back_k_ref[:, :128], preferred_element_type=f32)
    first_row = lax.broadcasted_iota(jnp.int32, (32, 128), 0) == 0
    for c in range(GC):
        mixed = jnp.dot(y_ref[c * pairs * 32 : (c + 1) * pairs * 32, :], back_k_ref[...], preferred_element_type=f32)
        for pair in range(pairs):
            row = c * 16 + 2 * pair
            line = lines[row : row + 1] + lines[row + 1 : row + 2]
            part = slice(pair * 128, (pair + 1) * 128)
            g_ref[c * 64 : c * 64 + 32, part] = mixed[pair * 32 : (pair + 1) * 32, 0:128].astype(bf16)
            g_ref[c * 64 + 32 : c * 64 + 64, part] = jnp.where(
                first_row, line, mixed[pair * 32 : (pair + 1) * 32, 128:256]
            ).astype(bf16)

    signed = lax.broadcasted_iota(jnp.int32, (P_SIZE, 256), 0)
    signed = jnp.where(signed < HALF, signed, signed - P_SIZE).astype(f32)
    for lane_at in range(0, pairs * 128, 256):
        part = slice(lane_at, lane_at + 256)
        all_scores = jnp.dot(back_l_ref[...], g_ref[:, part], preferred_element_type=f32)
        for c in range(GC):
            scores = all_scores[c * 64 : (c + 1) * 64]
            top = jnp.max(scores, axis=0, keepdims=True)
            weights = jnp.exp(scores - top)
            max_ref[c : c + 1, part] = top
            sum_ref[c : c + 1, part] = jnp.sum(weights, axis=0, keepdims=True)
            mom_ref[c : c + 1, part] = jnp.sum(weights * signed, axis=0, keepdims=True)

    lane = lax.broadcasted_iota(jnp.int32, (GC, 128), 1)
    left = lane < 64
    shift = lane % 64
    shift = jnp.where(shift < HALF, shift, shift - P_SIZE).astype(f32)
    place = lax.broadcasted_iota(jnp.int32, (GC, sections), 1)
    rows_out = jnp.zeros((GC, sections), f32)
    cols_out = jnp.zeros((GC, sections), f32)
    for pair in range(pairs):
        part = slice(pair * 128, (pair + 1) * 128)
        top = max_ref[:, part]
        top_a = jnp.max(jnp.where(left, top, -jnp.inf), axis=1, keepdims=True)
        top_b = jnp.max(jnp.where(left, -jnp.inf, top), axis=1, keepdims=True)
        factor = jnp.exp(top - jnp.where(left, top_a, top_b))
        total = factor * sum_ref[:, part]
        moment = factor * mom_ref[:, part]
        for k in range(2):
            mine = left if k == 0 else jnp.logical_not(left)
            den = jnp.sum(jnp.where(mine, total, 0.0), axis=1, keepdims=True)
            along_u = jnp.sum(jnp.where(mine, total * shift, 0.0), axis=1, keepdims=True)
            along_v = jnp.sum(jnp.where(mine, moment, 0.0), axis=1, keepdims=True)
            here = place == 2 * pair + k
            rows_out = jnp.where(here, along_u / den / 8.0, rows_out)
            cols_out = jnp.where(here, along_v / den / 8.0, cols_out)
    if not is_far:
        out_ref[0:GC, :] = rows_out
        out_ref[GC:, :] = cols_out
        return
    for component, mine in enumerate((rows_out, cols_out)):
        other = part_ref[component * GC : (component + 1) * GC, :]
        at = component * PATCHES
        out_ref[at : at + GC, :] = jnp.where(r == 0, mine, other)
        out_ref[at + GC : at + PATCHES, :] = jnp.where(r == 0, other, mine)


def call(kernel, name, out_shape, scratch, operands, flops, limit):
    smem = pl.BlockSpec(memory_space=pltpu.SMEM)
    vmem = pl.BlockSpec(memory_space=pltpu.VMEM)
    in_specs = [smem] + [vmem] * (len(operands) - 1)
    return pl.pallas_call(
        kernel,
        out_shape=out_shape,
        in_specs=in_specs,
        out_specs=tuple(vmem for _ in out_shape),
        scratch_shapes=scratch,
        compiler_params=pltpu.CompilerParams(vmem_limit_bytes=limit * 1024 * 1024),
        cost_estimate=pl.CostEstimate(flops=flops, bytes_accessed=0, transcendentals=0),
        name=name,
    )(*operands)


def make_tables(scalars):
    cols, rows, _, _ = make_constants()
    bf16 = jnp.bfloat16
    shapes = (
        jax.ShapeDtypeStruct((GR, 256 + GC * 16, 256), bf16),
        jax.ShapeDtypeStruct((PATCHES, 2 * WIN, 256), bf16),
    )
    return call(table_kernel, "make_tables", shapes, [], (scalars, cols, rows), 0, 16)


def measure_row(scalars, images, halo, prior, phalo, m_table, w_table, part=None):
    sections = images.shape[0]
    rows_x = (sections + 2) * 32 + 32
    _, _, back_k, back_l = make_constants()
    bf16 = jnp.bfloat16
    f32 = jnp.float32
    is_far = part is not None
    shapes = (jax.ShapeDtypeStruct((2 * (PATCHES if is_far else GC), sections), f32),)
    scratch = [
        pltpu.VMEM((GC, rows_x, 2 * WIN), bf16),
        pltpu.VMEM((GC, rows_x, 256), bf16),
        pltpu.VMEM((GC, 24, 256), f32),
        pltpu.VMEM((GC * (sections * 16 + 16), 256), bf16),
        pltpu.VMEM((256, sections * 64), bf16),
    ] + [pltpu.VMEM((GC, sections * 64), f32)] * 3
    operands = (scalars, images, halo, prior, phalo, m_table, w_table, back_k, back_l)
    operands = operands + ((part,) if is_far else ())
    name = "measure_far" if is_far else "measure_near"
    return call(partial(row_kernel, is_far), name, shapes, scratch, operands, 0, 24)[0]


def relaxed_step(extended):
    middle = extended[:, 1:-1]
    widened = jnp.pad(middle, ((0, 0), (0, 0), (1, 1), (0, 0)))
    beside = extended[:, :-2] + extended[:, 2:] + widened[:, :, :-2] + widened[:, :, 2:]
    return 0.5 * middle + 0.125 * beside


def earlier_groups(total):
    place = lax.axis_index("gz")
    count = lax.axis_size("gz")
    other = lax.ppermute(total, "gz", [(i, i ^ 1) for i in range(count)])
    pair = total + other
    across = lax.ppermute(pair, "gz", [(i, (i + 2) % count) for i in range(count)])
    return jnp.where(place >= 2, across, 0.0) + jnp.where(place % 2 == 1, other, 0.0)


def edge_rows(value, odd):
    top, bottom = value[:, :HALF], value[:, value.shape[1] - HALF :]
    return jnp.where(odd, bottom, top), jnp.where(odd, top, bottom)


def local(images, offsets, gaps):
    sections = images.shape[0]
    place = lax.axis_index("xy")
    last = lax.axis_size("xy") - 1
    odd = place % 2 == 1
    flags = jnp.stack([place == 0, place == last, lax.axis_index("gz") == 0, odd]).astype(jnp.int32)
    scalars = jnp.concatenate([flags, gaps, offsets.reshape(-1)])
    prior = ring(images[sections - 2 :], "gz", 1)
    far, near = edge_rows(images, odd)
    far, near = swap_far(far), swap_near(near)
    m_table, w_table, prior = lax.optimization_barrier((*make_tables(scalars), prior))
    pfar, pnear = edge_rows(prior, odd)
    pfar, pnear = swap_far(pfar), swap_near(pnear)
    part = measure_row(scalars, images, near, prior, pnear, m_table, w_table)
    measured = measure_row(scalars, images, far, prior, pfar, m_table, w_table, part)
    near = swap_near(measured)
    far = swap_far(measured)
    above = jnp.where(place == 0, 0.0, jnp.where(odd, near, far)).reshape(2, GR, GC, sections)
    below = jnp.where(place == last, 0.0, jnp.where(odd, far, near)).reshape(2, GR, GC, sections)
    measured = measured.reshape(2, GR, GC, sections)
    wide = relaxed_step(jnp.concatenate([above, measured, below], 1))
    row = place * GR + jnp.arange(-1, GR + 1)
    inside = (row >= 0) & (row < GR * (last + 1))
    wide = jnp.where(inside[None, :, None, None], wide, 0.0)
    smoothed = relaxed_step(wide)
    earlier_sum = earlier_groups(jnp.sum(smoothed, axis=3))
    triangle = jnp.triu(jnp.ones((sections, sections), jnp.float32))
    running = jnp.dot(smoothed.reshape(2 * PATCHES, sections), triangle, precision=lax.Precision.HIGHEST)
    running = lax.optimization_barrier(running)
    composed = running.reshape(smoothed.shape) + earlier_sum[..., None]
    return smoothed.transpose(0, 3, 1, 2), composed.transpose(0, 3, 1, 2)


def solution(mesh):
    in_specs = (P("gz", "xy", None), P("xy", None, None), P("gz"))
    out_specs = (P(None, "gz", "xy", None), P(None, "gz", "xy", None))
    return jax.shard_map(local, mesh=mesh, in_specs=in_specs, out_specs=out_specs, check_vma=False)
```

```python
from functools import partial
import math

import jax
import jax.numpy as jnp
import ml_dtypes
import numpy as np
from jax import lax
from jax.experimental import pallas as pl
from jax.experimental.pallas import tpu as pltpu
from jax.sharding import PartitionSpec as P

P_SIZE = 64
HALF = 32
SHARPNESS = 16.0
WIN = 128
GR = 2
GC = 4
PATCHES = GR * GC
AT_TOP, AT_BOTTOM, FIRST_GROUP, ODD, GAPS, OFFSETS = 0, 1, 2, 3, 4, 20


def ring(value, axis, steps):
    count = lax.axis_size(axis)
    return lax.ppermute(value, axis, [(source, (source + steps) % count) for source in range(count)])


def swap_near(value):
    count = lax.axis_size("xy")
    return lax.ppermute(value, "xy", [(i, i ^ 1) for i in range(count)])


def swap_far(value):
    count = lax.axis_size("xy")
    return lax.ppermute(value, "xy", [(i, (i + 1 if i % 2 else i - 1) % count) for i in range(count)])


def tables():
    indices = np.arange(P_SIZE)
    angles = (indices[:, None] * indices[None, :] % P_SIZE) * (2.0 * math.pi / P_SIZE)
    cos_t = np.cos(angles).astype(np.float32).astype(ml_dtypes.bfloat16).astype(np.float32)
    sin_t = np.sin(angles).astype(np.float32).astype(ml_dtypes.bfloat16).astype(np.float32)
    sin_t = np.where(np.abs(sin_t) < 1e-6, np.float32(0), sin_t)
    return cos_t, sin_t


def make_constants():
    cos_t, sin_t = tables()
    half = P_SIZE // 2
    cols = np.zeros((P_SIZE + 8, 256), np.float32)
    cols[:half, :P_SIZE] = cos_t[:half]
    cols[half:P_SIZE, :P_SIZE] = sin_t[:half]
    cols[P_SIZE:, :P_SIZE] = cos_t[half]
    rows = np.zeros((WIN, 2 * P_SIZE), np.float32)
    rows[:P_SIZE] = np.concatenate([cos_t, -sin_t], 1)
    to_re = np.concatenate([cos_t, -sin_t], 0)
    to_im = np.concatenate([sin_t, cos_t], 0)
    blank = np.zeros_like(to_re)
    back_k = np.concatenate(
        [
            np.concatenate([to_re, blank, to_im, blank], 1),
            np.concatenate([blank, to_re, blank, to_im], 1),
        ],
        0,
    )
    weight = np.where(np.arange(half) == 0, 1.0, 2.0).astype(np.float32)
    one = np.concatenate([cos_t[:, :half] * weight, -sin_t[:, :half] * weight], 1)
    one[:, half] = cos_t[:, half]
    scale = SHARPNESS / P_SIZE**4
    back_l = np.kron(np.eye(GC, dtype=np.float32), one * np.float32(scale))
    bf = ml_dtypes.bfloat16
    return cols, rows, back_k.astype(bf), back_l.astype(bf)


def table_kernel(scalar_ref, cols_ref, rows_ref, m_ref, w_ref):
    bf16 = jnp.bfloat16
    lane = lax.broadcasted_iota(jnp.int32, cols_ref.shape, 1)
    line = lax.broadcasted_iota(jnp.int32, (WIN, 128), 0)
    sign = jnp.where(lax.broadcasted_iota(jnp.int32, (WIN, 128), 1) < P_SIZE, 1.0, -1.0)
    for r in range(GR):
        inside_image = line >= jnp.where(scalar_ref[AT_TOP if r == 0 else AT_BOTTOM] == 1, HALF, 0)
        for c in range(GC):
            i = r * GC + c
            row_at = scalar_ref[OFFSETS + 2 * i] + r * HALF
            start = c * P_SIZE - HALF + scalar_ref[OFFSETS + 2 * i + 1]
            turn = jnp.where(start < 0, start + 256, start)
            turned = pltpu.roll(cols_ref[...], turn, 1)
            inside = (lane >= start) & (lane < start + P_SIZE)
            turned = jnp.where(inside, turned, 0.0)
            m_ref[r, c * 64 : (c + 1) * 64, :] = turned[:64].astype(bf16)
            m_ref[r, 256 + c * 16 : 256 + (c + 1) * 16, :] = jnp.concatenate([turned[64:]] * 2, 0).astype(bf16)
            straight = jnp.where(inside_image, pltpu.roll(rows_ref[...], row_at, 0), 0.0)
            crossed_over = pltpu.roll(straight, P_SIZE, 1)
            w_ref[i, 0:WIN, 0:128] = straight.astype(bf16)
            w_ref[i, 0:WIN, 128:256] = crossed_over.astype(bf16)
            w_ref[i, WIN:, 0:128] = (crossed_over * sign).astype(bf16)
            w_ref[i, WIN:, 128:256] = (straight * -sign).astype(bf16)


def crossed(partner_p, partner_q, own_p, own_q):
    left = lax.broadcasted_iota(jnp.int32, partner_p.shape, 1) < 64
    twice_re = jnp.where(left, partner_p, partner_q)
    twice_im = jnp.where(left, partner_q, -partner_p)
    return twice_re * own_p + twice_im * own_q


def gap_column(scalar_ref):
    row = lax.broadcasted_iota(jnp.int32, (16, 128), 0)
    gaps = jnp.ones((16, 128), jnp.int32)
    for s in range(16):
        gaps = jnp.where(row == s, scalar_ref[GAPS + s], gaps)
    return gaps


def cross_nyquist(i, own, prior, gaps, n_ref, y_ref, row):
    even = lax.broadcasted_iota(jnp.int32, (16, 128), 0) % 2 == 0
    n_ref[i, 8:24, :] = own
    n_ref[i, 0:8, :] = prior
    one_up = n_ref[i, 7:23, :]
    two_up = n_ref[i, 6:22, :]
    partner_p = jnp.where(gaps == 1, one_up[:, :128], two_up[:, :128])
    partner_q = jnp.where(gaps == 1, one_up[:, 128:], two_up[:, 128:])
    line = crossed(partner_p, partner_q, own[:, :128], own[:, 128:])
    y_ref[row : row + 16, 0:128] = jnp.where(even, line, 0.0).astype(jnp.bfloat16)
    y_ref[row : row + 16, 128:256] = jnp.where(even, 0.0, line).astype(jnp.bfloat16)


def row_kernel(
    is_far, scalar_ref, own_ref, halo_ref, prior_ref, phalo_ref, m_ref, w_ref, back_k_ref, back_l_ref, *rest
):
    if is_far:
        part_ref, *rest = rest
    out_ref, x_ref, z_ref, n_ref, y_ref, g_ref, max_ref, sum_ref, mom_ref = rest
    sections = own_ref.shape[0]
    stacked = sections + 2
    pairs = sections // 2
    f32 = jnp.float32
    bf16 = jnp.bfloat16
    main = stacked * 32
    r = scalar_ref[ODD] if is_far else 1 - scalar_ref[ODD]
    own_at = pl.multiple_of(r * HALF, HALF)
    has_prior = jnp.where(scalar_ref[FIRST_GROUP] == 1, 0.0, 1.0)

    def window(t):
        if t < 2:
            return [phalo_ref[t], prior_ref[t, pl.ds(own_at, WIN - HALF), :]]
        return [halo_ref[t - 2], own_ref[t - 2, pl.ds(own_at, WIN - HALF), :]]

    sub = lax.broadcasted_iota(jnp.int32, (8, WIN), 0)
    nyquist = [[jnp.zeros((8, WIN), f32) for _ in range(3)] for _ in range(GC)]
    for pair in range(stacked // 2):
        both = jnp.concatenate(window(2 * pair) + window(2 * pair + 1), 0)
        first = lax.dot_general(m_ref[r], both, (((1,), (1,)), ((), ())), preferred_element_type=f32)
        if pair == 0:
            first = first * has_prior
        for c in range(GC):
            for k in range(2):
                t = 2 * pair + k
                for half in range(2):
                    x_ref[c, t * 32 : (t + 1) * 32, half * WIN : (half + 1) * WIN] = first[
                        c * 64 + half * 32 : c * 64 + (half + 1) * 32, k * WIN : (k + 1) * WIN
                    ].astype(bf16)
                block, at = (2, t) if t < 2 else ((t - 2) // 8, (t - 2) % 8)
                line = first[256 + c * 16 : 264 + c * 16, k * WIN : (k + 1) * WIN]
                nyquist[c][block] = jnp.where(sub == at, line, nyquist[c][block])
    for c in range(GC):
        x_ref[c, main : main + 16, :WIN] = jnp.concatenate(nyquist[c][:2], 0).astype(bf16)
        x_ref[c, main + 16 :, :WIN] = jnp.concatenate([nyquist[c][2]] * 2, 0).astype(bf16)
        x_ref[c, main:, WIN:] = jnp.zeros((32, WIN), bf16)

    for c in range(GC):
        z_ref[c] = jnp.dot(x_ref[c], w_ref[r * GC + c], preferred_element_type=f32).astype(bf16)

    gaps = gap_column(scalar_ref)
    for c in range(GC):
        for s in range(sections):
            at = pl.multiple_of((s + 2 - scalar_ref[GAPS + s]) * 32, 32)
            row = (c * pairs + s // 2) * 32
            y_ref[row : row + 32, (s % 2) * 128 : (s % 2 + 1) * 128] = crossed(
                z_ref[c, pl.ds(at, 32), 0:128],
                z_ref[c, pl.ds(at, 32), 128:256],
                z_ref[c, (s + 2) * 32 : (s + 3) * 32, 0:128],
                z_ref[c, (s + 2) * 32 : (s + 3) * 32, 128:256],
            )
        own = z_ref[c, main : main + 16, :].astype(f32)
        prior = pltpu.roll(z_ref[c, main + 16 : main + 32, :].astype(f32)[0:8], 6, 0)
        cross_nyquist(c, own, prior, gaps, n_ref, y_ref, GC * pairs * 32 + c * 16)

    lines = jnp.dot(y_ref[GC * pairs * 32 :, :], back_k_ref[:, :128], preferred_element_type=f32)
    first_row = lax.broadcasted_iota(jnp.int32, (32, 128), 0) == 0
    for c in range(GC):
        mixed = jnp.dot(y_ref[c * pairs * 32 : (c + 1) * pairs * 32, :], back_k_ref[...], preferred_element_type=f32)
        for pair in range(pairs):
            row = c * 16 + 2 * pair
            line = lines[row : row + 1] + lines[row + 1 : row + 2]
            part = slice(pair * 128, (pair + 1) * 128)
            g_ref[c * 64 : c * 64 + 32, part] = mixed[pair * 32 : (pair + 1) * 32, 0:128].astype(bf16)
            g_ref[c * 64 + 32 : c * 64 + 64, part] = jnp.where(
                first_row, line, mixed[pair * 32 : (pair + 1) * 32, 128:256]
            ).astype(bf16)

    signed = lax.broadcasted_iota(jnp.int32, (P_SIZE, 256), 0)
    signed = jnp.where(signed < HALF, signed, signed - P_SIZE).astype(f32)
    for lane_at in range(0, pairs * 128, 256):
        part = slice(lane_at, lane_at + 256)
        all_scores = jnp.dot(back_l_ref[...], g_ref[:, part], preferred_element_type=f32)
        for c in range(GC):
            scores = all_scores[c * 64 : (c + 1) * 64]
            top = jnp.max(scores, axis=0, keepdims=True)
            weights = jnp.exp(scores - top)
            total = jnp.sum(weights, axis=0, keepdims=True)
            moment = jnp.sum(weights * signed, axis=0, keepdims=True)
            for k in range(2):
                row = (lane_at // 128 + k) * GC + c
                max_ref[row : row + 1, :] = top[:, k * 128 : (k + 1) * 128]
                sum_ref[row : row + 1, :] = total[:, k * 128 : (k + 1) * 128]
                mom_ref[row : row + 1, :] = moment[:, k * 128 : (k + 1) * 128]

    lane = lax.broadcasted_iota(jnp.int32, (pairs * GC, 128), 1)
    pair_of_row = lax.broadcasted_iota(jnp.int32, (pairs * GC, 128), 0) // GC
    left = lane < 64
    shift = lane % 64
    shift = jnp.where(shift < HALF, shift, shift - P_SIZE).astype(f32)
    top = max_ref[...]
    top_a = jnp.max(jnp.where(left, top, -jnp.inf), axis=1, keepdims=True)
    top_b = jnp.max(jnp.where(left, -jnp.inf, top), axis=1, keepdims=True)
    factor = jnp.exp(top - jnp.where(left, top_a, top_b))
    total = factor * sum_ref[...]
    moment = factor * mom_ref[...]
    along = total * shift
    rows_out = jnp.zeros((pairs * GC, 128), f32)
    cols_out = jnp.zeros((pairs * GC, 128), f32)
    for k in range(2):
        mine = left if k == 0 else jnp.logical_not(left)
        den = jnp.sum(jnp.where(mine, total, 0.0), axis=1, keepdims=True) * 8.0
        along_u = jnp.sum(jnp.where(mine, along, 0.0), axis=1, keepdims=True)
        along_v = jnp.sum(jnp.where(mine, moment, 0.0), axis=1, keepdims=True)
        here = lane == 2 * pair_of_row + k
        rows_out = jnp.where(here, along_u / den, rows_out)
        cols_out = jnp.where(here, along_v / den, cols_out)

    def gather_rows(value):
        value = sum(value[at : at + 8] for at in range(0, pairs * GC, 8))
        return (value[0:GC] + value[GC:])[:, :sections]

    rows_out, cols_out = gather_rows(rows_out), gather_rows(cols_out)
    if not is_far:
        out_ref[0:GC, :] = rows_out
        out_ref[GC:, :] = cols_out
        return
    for component, mine in enumerate((rows_out, cols_out)):
        other = part_ref[component * GC : (component + 1) * GC, :]
        at = component * PATCHES
        out_ref[at : at + GC, :] = jnp.where(r == 0, mine, other)
        out_ref[at + GC : at + PATCHES, :] = jnp.where(r == 0, other, mine)


def call(kernel, name, out_shape, scratch, operands, flops, limit):
    smem = pl.BlockSpec(memory_space=pltpu.SMEM)
    vmem = pl.BlockSpec(memory_space=pltpu.VMEM)
    in_specs = [smem] + [vmem] * (len(operands) - 1)
    return pl.pallas_call(
        kernel,
        out_shape=out_shape,
        in_specs=in_specs,
        out_specs=tuple(vmem for _ in out_shape),
        scratch_shapes=scratch,
        compiler_params=pltpu.CompilerParams(vmem_limit_bytes=limit * 1024 * 1024),
        cost_estimate=pl.CostEstimate(flops=flops, bytes_accessed=0, transcendentals=0),
        name=name,
    )(*operands)


def make_tables(scalars):
    cols, rows, _, _ = make_constants()
    bf16 = jnp.bfloat16
    shapes = (
        jax.ShapeDtypeStruct((GR, 256 + GC * 16, 256), bf16),
        jax.ShapeDtypeStruct((PATCHES, 2 * WIN, 256), bf16),
    )
    return call(table_kernel, "make_tables", shapes, [], (scalars, cols, rows), 0, 16)


def measure_row(scalars, images, halo, prior, phalo, m_table, w_table, part=None):
    sections = images.shape[0]
    rows_x = (sections + 2) * 32 + 32
    _, _, back_k, back_l = make_constants()
    bf16 = jnp.bfloat16
    f32 = jnp.float32
    is_far = part is not None
    shapes = (jax.ShapeDtypeStruct((2 * (PATCHES if is_far else GC), sections), f32),)
    scratch = [
        pltpu.VMEM((GC, rows_x, 2 * WIN), bf16),
        pltpu.VMEM((GC, rows_x, 256), bf16),
        pltpu.VMEM((GC, 24, 256), f32),
        pltpu.VMEM((GC * (sections * 16 + 16), 256), bf16),
        pltpu.VMEM((256, sections * 64), bf16),
    ] + [pltpu.VMEM((sections // 2 * GC, 128), f32)] * 3
    operands = (scalars, images, halo, prior, phalo, m_table, w_table, back_k, back_l)
    operands = operands + ((part,) if is_far else ())
    name = "measure_far" if is_far else "measure_near"
    return call(partial(row_kernel, is_far), name, shapes, scratch, operands, 0, 24)[0]


def relaxed_step(extended):
    middle = extended[:, 1:-1]
    widened = jnp.pad(middle, ((0, 0), (0, 0), (1, 1), (0, 0)))
    beside = extended[:, :-2] + extended[:, 2:] + widened[:, :, :-2] + widened[:, :, 2:]
    return 0.5 * middle + 0.125 * beside


def earlier_groups(total):
    place = lax.axis_index("gz")
    count = lax.axis_size("gz")
    other = lax.ppermute(total, "gz", [(i, i ^ 1) for i in range(count)])
    pair = total + other
    across = lax.ppermute(pair, "gz", [(i, (i + 2) % count) for i in range(count)])
    return jnp.where(place >= 2, across, 0.0) + jnp.where(place % 2 == 1, other, 0.0)


def edge_rows(value, odd):
    top, bottom = value[:, :HALF], value[:, value.shape[1] - HALF :]
    return jnp.where(odd, bottom, top), jnp.where(odd, top, bottom)


def local(images, offsets, gaps):
    sections = images.shape[0]
    place = lax.axis_index("xy")
    last = lax.axis_size("xy") - 1
    odd = place % 2 == 1
    flags = jnp.stack([place == 0, place == last, lax.axis_index("gz") == 0, odd]).astype(jnp.int32)
    scalars = jnp.concatenate([flags, gaps, offsets.reshape(-1)])
    prior = ring(images[sections - 2 :], "gz", 1)
    far, near = edge_rows(images, odd)
    far, near = swap_far(far), swap_near(near)
    m_table, w_table, images = lax.optimization_barrier((*make_tables(scalars), images))
    pfar, pnear = edge_rows(prior, odd)
    pfar, pnear = swap_far(pfar), swap_near(pnear)
    part = measure_row(scalars, images, near, prior, pnear, m_table, w_table)
    measured = measure_row(scalars, images, far, prior, pfar, m_table, w_table, part)
    near = swap_near(measured)
    far = swap_far(measured)
    above = jnp.where(place == 0, 0.0, jnp.where(odd, near, far)).reshape(2, GR, GC, sections)
    below = jnp.where(place == last, 0.0, jnp.where(odd, far, near)).reshape(2, GR, GC, sections)
    measured = measured.reshape(2, GR, GC, sections)
    wide = relaxed_step(jnp.concatenate([above, measured, below], 1))
    row = place * GR + jnp.arange(-1, GR + 1)
    inside = (row >= 0) & (row < GR * (last + 1))
    wide = jnp.where(inside[None, :, None, None], wide, 0.0)
    smoothed = relaxed_step(wide)
    earlier_sum = earlier_groups(jnp.sum(smoothed, axis=3))
    triangle = jnp.triu(jnp.ones((sections, sections), jnp.float32))
    running = jnp.dot(smoothed.reshape(2 * PATCHES, sections), triangle, precision=lax.Precision.HIGHEST)
    running = lax.optimization_barrier(running)
    composed = running.reshape(smoothed.shape) + earlier_sum[..., None]
    return smoothed.transpose(0, 3, 1, 2), composed.transpose(0, 3, 1, 2)


def solution(mesh):
    in_specs = (P("gz", "xy", None), P("xy", None, None), P("gz"))
    out_specs = (P(None, "gz", "xy", None), P(None, "gz", "xy", None))
    return jax.shard_map(local, mesh=mesh, in_specs=in_specs, out_specs=out_specs, check_vma=False)
```
